512 devices in a mesh: tm: 16 (over z), height: 8 (over y, core), width: 4 (over x).
Axes of the slice: x: 4, y: 4, z: 16, core: 2. Of those that a mesh axis runs over, the one named last changes fastest.
Arguments:
- latent: bfloat16 [32, 16, 64, 384], P('tm', 'height', 'width'), may hold values from -6 to 6
- norm_gain: float32 [384], replicated, may hold values from 0.1 to 1.9
- conv_weight: bfloat16 [3, 3, 3, 384, 384], P(None, None, None, None, 'tm'), may hold values from -0.0625 to 0.0625
- attn_gain: float32 [384], replicated, may hold values from 0.1 to 1.9
- w_qkv: bfloat16 [384, 1152], replicated, may hold values from -3 to 3
- w_out: bfloat16 [384, 384], replicated, may hold values from -0.3125 to 0.3125
Outputs:
- decoded: bfloat16 [32, 16, 64, 384], P('tm', 'height', 'width')
The draws below stay inside these ranges and needn't reach their ends.
All inputs are finite; a program needn't handle non-finite values.
Results may differ from the reference program's by a relative error of at most 0.013.
Values may be sent and summed in bfloat16 or wider, within the bound.
No kernel may reach another device: no remote copies, remote signals or barrier semaphores. Data moves between devices by JAX's collectives and lax.ppermute only.
A program may use at most 64 MiB of HBM per device.

```python
import math
import jax
import jax.numpy as jnp
from jax import lax

C = 384
FRAMES = 32
ROWS = 16
COLS = 64


def draw_w_qkv(key, part):
    key = jax.random.fold_in(key, 7)
    first = jax.random.fold_in(key, 0)
    second = jax.random.fold_in(key, 1)
    fourth = jax.random.fold_in(key, 3)
    factor = 1.73 / math.sqrt(C)
    query_part = jax.random.normal(first, (C, C), jnp.float32) * factor
    key_part = jax.random.normal(second, (C, C), jnp.float32) * factor
    value_part = jax.random.normal(fourth, (C, C), jnp.float32) / math.sqrt(C)
    whole = jnp.concatenate([query_part, key_part, value_part], axis=1)
    return jnp.clip(whole, -3.0, 3.0).astype(jnp.bfloat16)


def shard_levels(key, extent, cuts, least, high):
    def one(dim, shards_of):
        draws = jax.random.uniform(jax.random.fold_in(jax.random.fold_in(key, 6), dim), (shards_of,), jnp.float32, least / len(cuts), high / len(cuts))
        return jnp.repeat(jnp.exp(draws), extent[dim] // shards_of).reshape((-1,) + (1,) * (len(extent) - dim - 1))

    level = one(*cuts[0])
    for cut in cuts[1:]:
        level = level * one(*cut)
    return level


def noise(stream_key, dims, deviation, bound, cuts=(), held_as=jnp.bfloat16):
    array = deviation * jax.random.normal(stream_key, dims, jnp.float32)
    if cuts:
        array = array * shard_levels(stream_key, dims, cuts, -0.22, 0.18)
    return jnp.clip(array, -bound, bound).astype(held_as)


def setup_inputs(seed: int = 0) -> dict:
    streams_of = jax.random.split(jax.random.key(seed), 7)
    return {
        "latent": noise(streams_of[0], (FRAMES, ROWS, COLS, C), 1.0, 6.0, ((0, 16), (1, 8), (2, 4))),
        "norm_gain": jnp.clip(1.0 + 0.18 * jax.random.normal(streams_of[1], (C,), jnp.float32), 0.1, 1.9),
        "conv_weight": noise(streams_of[2], (3, 3, 3, C, C), (27 * C) ** -0.5, 0.0625, ((4, 16),)),
        "attn_gain": jnp.clip(1.0 + 0.18 * jax.random.normal(streams_of[3], (C,), jnp.float32), 0.1, 1.9),
        "w_qkv": draw_w_qkv(jax.random.fold_in(streams_of[6], 71), 0),
        "w_out": noise(streams_of[5], (C, C), C ** -0.5, 0.3125),
    }


def rms_scale(values, gain):
    mean_sq = lax.optimization_barrier(jnp.mean(values * values, axis=-1, keepdims=True))
    return values * lax.rsqrt(mean_sq + 1e-06) * gain

def frame_attention(query_rows, key_rows, value_rows):
    scores = jnp.dot(query_rows, key_rows.T, preferred_element_type=jnp.float32) / jnp.sqrt(jnp.float32(C))
    peaks = lax.optimization_barrier(jnp.max(scores, axis=-1, keepdims=True))
    powers = jnp.exp(scores - peaks)
    total = lax.optimization_barrier(jnp.sum(powers, axis=-1, keepdims=True))
    mixed = jnp.dot(powers.astype(jnp.bfloat16), value_rows, preferred_element_type=jnp.float32)
    return (mixed / total).astype(jnp.bfloat16)

def reference(latent, norm_gain, conv_weight, attn_gain, w_qkv, w_out):
    latent_f = latent.astype(jnp.float32)
    activated = jax.nn.silu(rms_scale(latent_f, norm_gain)).astype(jnp.bfloat16)
    padded = jnp.pad(activated, ((2, 0), (1, 1), (1, 1), (0, 0)))
    conv_out = jnp.zeros((FRAMES * ROWS * COLS, C), jnp.float32)
    for time_tap in range(3):
        for row_tap in range(3):
            for col_tap in range(3):
                window = padded[time_tap:time_tap + FRAMES, row_tap:row_tap + ROWS, col_tap:col_tap + COLS]
                conv_out = conv_out + jnp.dot(window.reshape(-1, C), conv_weight[time_tap, row_tap, col_tap], preferred_element_type=jnp.float32)
    hidden = (latent_f + conv_out.reshape(FRAMES, ROWS, COLS, C)).astype(jnp.bfloat16)
    normed = rms_scale(hidden.astype(jnp.float32), attn_gain).astype(jnp.bfloat16)
    projected = jnp.dot(normed.reshape(-1, C), w_qkv, preferred_element_type=jnp.float32)
    projected = projected.astype(jnp.bfloat16).reshape(FRAMES, ROWS * COLS, 3 * C)
    query_all = projected[:, :, :C]
    key_all = projected[:, :, C:2 * C]
    value_all = projected[:, :, 2 * C:]
    attended = lax.map(lambda trio: frame_attention(trio[0], trio[1], trio[2]), (query_all, key_all, value_all))
    update = jnp.dot(attended.reshape(-1, C), w_out, preferred_element_type=jnp.float32)
    decoded = hidden.astype(jnp.float32) + update.reshape(FRAMES, ROWS, COLS, C)
    return decoded.astype(jnp.bfloat16)
```

```python
import functools

import jax
import jax.numpy as jnp
from jax import lax
from jax.experimental import pallas as pl
from jax.experimental.pallas import tpu as pltpu
from jax.sharding import Mesh, PartitionSpec as P

F32 = jnp.float32
BF16 = jnp.bfloat16
TAPS = 27
GROUP = 24
SLOT = 32
DEPTH = 896
PLANE = ("y", "width")
VMEM = pl.BlockSpec(memory_space=pltpu.VMEM)
SMEM = pl.BlockSpec(memory_space=pltpu.SMEM)
LIMIT = 48 * 1024 * 1024


def call(body, out, specs, flops=1_000_000, moved=1_000_000, scratch=()):
    many = isinstance(out, (tuple, list))
    return pl.pallas_call(
        body,
        out_shape=out,
        in_specs=specs,
        out_specs=[VMEM] * len(out) if many else VMEM,
        scratch_shapes=list(scratch),
        compiler_params=pltpu.CompilerParams(vmem_limit_bytes=LIMIT),
        cost_estimate=pl.CostEstimate(flops=flops, bytes_accessed=moved, transcendentals=0),
    )


def rms_scale(values, gain):
    mean_sq = jnp.mean(values * values, axis=-1, keepdims=True)
    return values * lax.rsqrt(mean_sq + 1e-06) * gain


def weight_body(chip_ref, weight_ref, out_ref):
    start = chip_ref[0] * GROUP
    source = lax.broadcasted_iota(jnp.int32, (384, 128), 0)
    target = lax.broadcasted_iota(jnp.int32, (384, 128), 1)
    tiles = [jnp.zeros((GROUP, 128), F32) for _ in range(7)]
    for place in range(4):
        offset = target - place * SLOT
        wanted = (offset >= 0) & (offset < GROUP) & (source == start + offset)
        pick = wanted.astype(F32).astype(BF16)
        for tile in range(7):
            tap = tile * 4 + place
            if tap < TAPS:
                tiles[tile] += jnp.dot(weight_ref[tap], pick, preferred_element_type=F32)
    for tile in range(7):
        value = tiles[tile].astype(BF16)
        for plane in range(out_ref.shape[0]):
            out_ref[plane, :, tile * 128 : tile * 128 + 128] = value


def activate_body(before_ref, now_ref, gain_ref, out_ref):
    gain = gain_ref[...]
    halves = []
    for ref in (before_ref, now_ref):
        scaled = rms_scale(ref[...].astype(F32), gain)
        halves.append(scaled / (1.0 + jnp.exp(-scaled)))
    turned = jnp.concatenate(halves, axis=0).T
    later = pltpu.roll(turned, 96, 1)
    blank = jnp.zeros((SLOT - GROUP, 128), F32)
    for core, whole in ((0, turned), (1, later)):
        for chip in range(16):
            block = jnp.concatenate([whole[chip * GROUP : chip * GROUP + GROUP], blank], axis=0)
            out_ref[chip // 4, core, chip % 4] = block.astype(BF16)


def patch_body(cells_ref, out_ref):
    source = lax.broadcasted_iota(jnp.int32, (128, 384), 0)
    target = lax.broadcasted_iota(jnp.int32, (128, 384), 1)
    frame, row, col = source // 32, (source // 16) % 2, source % 16
    lane = lax.broadcasted_iota(jnp.int32, (256, 128), 1)
    grid = jnp.zeros((256, 384), F32)
    for width in range(4):
        place = (frame < 3) & (target == frame * 128 + row * 64 + width * 16 + col)
        rows = jnp.concatenate([cells_ref[height, width] for height in range(8)], axis=0)
        grid += jnp.dot(rows, place.astype(F32).astype(BF16), preferred_element_type=F32)
    blank = jnp.zeros((SLOT, 128), F32)
    for time_tap in range(3):
        still = grid[:, time_tap * 128 : time_tap * 128 + 128]
        left = jnp.where(lane % 64 == 0, 0.0, pltpu.roll(still, 1, 1))
        right = jnp.where(lane % 64 == 63, 0.0, pltpu.roll(still, 127, 1))
        for col_tap, base in enumerate((left, still, right)):
            swapped = pltpu.roll(base, 64, 1)
            above = jnp.concatenate([blank, swapped[:-SLOT]], axis=0)
            below = jnp.concatenate([swapped[SLOT:], blank], axis=0)
            up = jnp.where(lane < 64, above, swapped)
            down = jnp.where(lane < 64, swapped, below)
            for row_tap, value in enumerate((up, base, down)):
                tap = (time_tap * 3 + row_tap) * 3 + col_tap
                value = value.astype(BF16)
                for height in range(8):
                    out_ref[tap * SLOT : tap * SLOT + SLOT, height * 128 : height * 128 + 128] = value[
                        height * SLOT : height * SLOT + SLOT
                    ]
    out_ref[TAPS * SLOT :, :] = jnp.zeros((DEPTH - TAPS * SLOT, 1024), BF16)


def conv_body(patch_ref, weight_ref, out_ref):
    for part in range(4):
        turned = jnp.dot(
            weight_ref[...], patch_ref[:, part * 256 : part * 256 + 256], preferred_element_type=F32
        )
        summed = turned.T.astype(BF16)
        for row in range(4):
            for width in range(4):
                out_ref[part * 4 + width, row * 16 : row * 16 + 16, :] = summed[
                    row * 64 + width * 16 : row * 64 + width * 16 + 16
                ]


def hidden_body(part_ref, latent_ref, gain_ref, hidden_ref, normed_ref):
    summed = latent_ref[...].astype(F32)
    for source in range(16):
        summed += part_ref[source].astype(F32)
    hidden = summed.astype(BF16)
    hidden_ref[...] = hidden
    normed = rms_scale(hidden.astype(F32), gain_ref[...]).astype(BF16)
    for target in range(16):
        normed_ref[target] = normed


def query_body(normed_ref, w_ref, out_ref):
    query = jnp.dot(normed_ref[0], w_ref[:, :384], preferred_element_type=F32).astype(BF16)
    out_ref[...] = lax.dot_general(
        query, w_ref[:, 384:768], (((1,), (1,)), ((), ())), preferred_element_type=F32
    ).astype(BF16)


def attend_body(core_ref, query_ref, cells_ref, hidden_ref, w_ref, w_out_ref, keep_ref, send_ref):
    cells = cells_ref[...]
    scores = lax.dot_general(
        query_ref[...], cells, (((1,), (1,)), ((), ())), preferred_element_type=F32
    ) * (1.0 / 384.0**0.5)
    powers = jnp.exp(scores - jnp.max(scores, axis=-1, keepdims=True))
    total = jnp.sum(powers, axis=-1, keepdims=True)
    mixed = jnp.dot(powers.astype(BF16), cells, preferred_element_type=F32) / total
    attended = jnp.dot(mixed.astype(BF16), w_ref[:, 768:], preferred_element_type=F32)
    update = jnp.dot(attended.astype(BF16), w_out_ref[...], preferred_element_type=F32)
    decoded = (hidden_ref[...].astype(F32) + update).astype(BF16)
    first = core_ref[0] == 0
    keep_ref[...] = jnp.where(first, decoded[:32], decoded[32:])
    send_ref[...] = jnp.where(first, decoded[32:], decoded[:32])


def local(latent, norm_gain, conv_weight, attn_gain, w_qkv, w_out):
    channels = 384
    core = lax.axis_index("core")
    chip = lax.axis_index("y") * 4 + lax.axis_index("width")
    swap = [(0, 1), (1, 0)]
    shape = jax.ShapeDtypeStruct
    with jax.named_scope("weight_slices"):
        turned = jnp.transpose(conv_weight.reshape(TAPS, channels, GROUP), (0, 2, 1))
        pieces = call(weight_body, shape((16, GROUP, DEPTH), BF16), [SMEM, VMEM])(
            chip.astype(jnp.int32).reshape(1), turned
        )
        weight = lax.all_to_all(pieces, "tm", 0, 0).reshape(channels, DEPTH)
    with jax.named_scope("earlier_frames"):
        cells = latent.reshape(64, channels)
        before = lax.ppermute(cells, "tm", [(i, i + 1) for i in range(15)])
    with jax.named_scope("activated"):
        blocks = call(activate_body, shape((4, 2, 4, SLOT, 128), BF16), [VMEM] * 3)(
            before, cells, norm_gain.reshape(1, channels)
        )
        blocks = lax.all_to_all(blocks.reshape(32, SLOT, 128), ("y", "core", "width"), 0, 0)
        patches = call(patch_body, shape((DEPTH, 1024), BF16), [VMEM])(blocks.reshape(8, 4, SLOT, 128))
    with jax.named_scope("own_latent"):
        first = core == 0
        kept = jnp.where(first, cells[:32], cells[32:])
        other = lax.ppermute(jnp.where(first, cells[32:], cells[:32]), "core", swap)
        own = jnp.where(first, jnp.concatenate([kept, other]), jnp.concatenate([other, kept]))
    with jax.named_scope("conv"):
        parts = call(conv_body, shape((16, 64, channels), BF16), [VMEM] * 2, 700_000_000)(patches, weight)
        parts = lax.all_to_all(parts, PLANE, 0, 0)
    with jax.named_scope("hidden"):
        hidden, normed = call(
            hidden_body, [shape((64, channels), BF16), shape((16, 64, channels), BF16)], [VMEM] * 3
        )(parts, own, attn_gain.reshape(1, channels))
    with jax.named_scope("keys"):
        gathered = lax.all_to_all(normed, PLANE, 0, 0).reshape(1024, channels)
    with jax.named_scope("query"):
        query = call(query_body, shape((64, channels), BF16), [VMEM] * 2, 40_000_000)(normed, w_qkv)
    with jax.named_scope("attention"):
        half = shape((32, channels), BF16)
        keep, send = call(attend_body, [half, half], [SMEM] + [VMEM] * 5, 200_000_000)(
            core.astype(jnp.int32).reshape(1), query, gathered, hidden, w_qkv, w_out
        )
        other = lax.ppermute(send, "core", swap)
        out = jnp.where(first, jnp.concatenate([keep, other]), jnp.concatenate([other, keep]))
    return out.reshape(latent.shape)


def solution(mesh):
    devices = mesh.devices.reshape(16, 4, 2, 4)
    fine = Mesh(devices, ("tm", "y", "core", "width"))
    cells = P("tm", ("y", "core"), "width", None)
    in_specs = (cells, P(), P(None, None, None, None, "tm"), P(), P(), P())
    return jax.shard_map(local, mesh=fine, in_specs=in_specs, out_specs=cells, check_vma=False)
```

```python
import functools

import jax
import jax.numpy as jnp
from jax import lax
from jax.experimental import pallas as pl
from jax.experimental.pallas import tpu as pltpu
from jax.sharding import Mesh, PartitionSpec as P

F32 = jnp.float32
BF16 = jnp.bfloat16
TAPS = 27
GROUP = 24
HALF = 14
DEPTH = 384
PLANE = ("y", "width")
VMEM = pl.BlockSpec(memory_space=pltpu.VMEM)
SMEM = pl.BlockSpec(memory_space=pltpu.SMEM)
LIMIT = 24 * 1024 * 1024


def call(body, out, specs, flops=1_000_000, moved=1_000_000, scratch=()):
    many = isinstance(out, (tuple, list))
    return pl.pallas_call(
        body,
        out_shape=out,
        in_specs=specs,
        out_specs=[VMEM] * len(out) if many else VMEM,
        scratch_shapes=list(scratch),
        compiler_params=pltpu.CompilerParams(vmem_limit_bytes=LIMIT),
        cost_estimate=pl.CostEstimate(flops=flops, bytes_accessed=moved, transcendentals=0),
    )


def rms_scale(values, gain):
    mean_sq = jnp.mean(values * values, axis=-1, keepdims=True)
    return values * lax.rsqrt(mean_sq + 1e-06) * gain


def weight_body(place_ref, weight_ref, out_ref):
    start = place_ref[0] * GROUP
    first_tap = place_ref[1] * HALF
    source = lax.broadcasted_iota(jnp.int32, (384, 128), 0)
    target = lax.broadcasted_iota(jnp.int32, (384, 128), 1)
    pick = ((target < GROUP) & (source == start + target)).astype(F32).astype(BF16)
    rows = [weight_ref[jnp.minimum(first_tap + tap, TAPS - 1)] for tap in range(HALF)]
    picked = jnp.dot(jnp.concatenate(rows, axis=0), pick, preferred_element_type=F32)
    lane = lax.broadcasted_iota(jnp.int32, (GROUP, 128), 1)
    tiles = [jnp.zeros((GROUP, 128), F32) for _ in range(3)]
    for tap in range(HALF):
        value = picked[tap * GROUP : tap * GROUP + GROUP]
        if tap == HALF - 1:
            value = jnp.where(first_tap + tap < TAPS, value, 0.0)
        tile, offset = divmod(tap * GROUP, 128)
        value = pltpu.roll(value, offset, 1) if offset else value
        if offset + GROUP > 128:
            tiles[tile] += jnp.where(lane >= offset, value, 0.0)
            tiles[tile + 1] += jnp.where(lane < offset, value, 0.0)
        else:
            tiles[tile] += value
    whole = jnp.concatenate(tiles, axis=1).astype(BF16)
    for plane in range(16):
        out_ref[plane] = whole


def activate_body(before_ref, now_ref, gain_ref, out_ref):
    gain = gain_ref[...]
    halves = []
    for ref in (before_ref, now_ref):
        scaled = rms_scale(ref[...].astype(F32), gain)
        halves.append(scaled / (1.0 + jnp.exp(-scaled)))
    turned = jnp.concatenate(halves, axis=0).T
    later = pltpu.roll(turned, 96, 1)
    for core, whole in ((0, turned), (1, later)):
        for chip in range(16):
            out_ref[chip // 4, core, chip % 4] = whole[chip * GROUP : chip * GROUP + GROUP].astype(BF16)


def patch_body(cells_ref, out_ref, held_ref):
    source = lax.broadcasted_iota(jnp.int32, (128, 384), 0)
    target = lax.broadcasted_iota(jnp.int32, (128, 384), 1)
    frame, row, col = source // 32, (source // 16) % 2, source % 16
    lane = lax.broadcasted_iota(jnp.int32, (8 * GROUP, 128), 1)
    grid = jnp.zeros((8 * GROUP, 384), F32)
    for width in range(4):
        place = (frame < 3) & (target == frame * 128 + row * 64 + width * 16 + col)
        rows = jnp.concatenate([cells_ref[height, width].astype(F32) for height in range(8)], axis=0)
        grid += jnp.dot(rows.astype(BF16), place.astype(F32).astype(BF16), preferred_element_type=F32)
    blank = jnp.zeros((GROUP, 128), F32)
    for time_tap in range(3):
        still = grid[:, time_tap * 128 : time_tap * 128 + 128]
        left = jnp.where(lane % 64 == 0, 0.0, pltpu.roll(still, 1, 1))
        right = jnp.where(lane % 64 == 63, 0.0, pltpu.roll(still, 127, 1))
        for col_tap, base in enumerate((left, still, right)):
            swapped = pltpu.roll(base, 64, 1)
            above = jnp.concatenate([blank, swapped[:-GROUP]], axis=0)
            below = jnp.concatenate([swapped[GROUP:], blank], axis=0)
            up = jnp.where(lane < 64, above, swapped)
            down = jnp.where(lane < 64, swapped, below)
            for row_tap, value in enumerate((up, base, down)):
                half, tap = divmod((time_tap * 3 + row_tap) * 3 + col_tap, HALF)
                for height in range(8):
                    held_ref[
                        half, tap * GROUP : tap * GROUP + GROUP, height * 128 : height * 128 + 128
                    ] = value[height * GROUP : height * GROUP + GROUP]
    held_ref[0, HALF * GROUP :, :] = jnp.zeros((DEPTH - HALF * GROUP, 1024), F32)
    held_ref[1, (TAPS - HALF) * GROUP :, :] = jnp.zeros((DEPTH - (TAPS - HALF) * GROUP, 1024), F32)
    out_ref[...] = held_ref[...].astype(BF16)


def conv_body(place_ref, patch_ref, mine_ref, other_ref, out_ref):
    core = place_ref[1]
    for part in range(4):
        cut = slice(part * 256, part * 256 + 256)
        turned = jnp.dot(mine_ref[...], patch_ref[core, :, cut], preferred_element_type=F32)
        turned += jnp.dot(other_ref[...], patch_ref[1 - core, :, cut], preferred_element_type=F32)
        summed = turned.T.astype(BF16)
        for row in range(4):
            for width in range(4):
                out_ref[part * 4 + width, row * 16 : row * 16 + 16, :] = summed[
                    row * 64 + width * 16 : row * 64 + width * 16 + 16
                ]


def hidden_body(part_ref, latent_ref, gain_ref, hidden_ref, normed_ref):
    summed = latent_ref[...].astype(F32)
    for source in range(16):
        summed += part_ref[source].astype(F32)
    hidden = summed.astype(BF16)
    hidden_ref[...] = hidden
    normed = rms_scale(hidden.astype(F32), gain_ref[...]).astype(BF16)
    for target in range(16):
        normed_ref[target] = normed


def query_body(normed_ref, w_ref, out_ref):
    query = jnp.dot(normed_ref[0], w_ref[:, :384], preferred_element_type=F32).astype(BF16)
    out_ref[...] = lax.dot_general(
        query, w_ref[:, 384:768], (((1,), (1,)), ((), ())), preferred_element_type=F32
    ).astype(BF16)


def attend_body(place_ref, query_ref, cells_ref, hidden_ref, w_ref, w_out_ref, keep_ref, send_ref):
    cells = cells_ref[...]
    scores = lax.dot_general(
        query_ref[...], cells, (((1,), (1,)), ((), ())), preferred_element_type=F32
    ) * (1.0 / 384.0**0.5)
    powers = jnp.exp(scores - jnp.max(scores, axis=-1, keepdims=True))
    total = jnp.sum(powers, axis=-1, keepdims=True)
    mixed = jnp.dot(powers.astype(BF16), cells, preferred_element_type=F32) / total
    attended = jnp.dot(mixed.astype(BF16), w_ref[:, 768:], preferred_element_type=F32)
    update = jnp.dot(attended.astype(BF16), w_out_ref[...], preferred_element_type=F32)
    decoded = (hidden_ref[...].astype(F32) + update).astype(BF16)
    first = place_ref[1] == 0
    keep_ref[...] = jnp.where(first, decoded[:32], decoded[32:])
    send_ref[...] = jnp.where(first, decoded[32:], decoded[:32])


def local(latent, norm_gain, conv_weight, attn_gain, w_qkv, w_out):
    channels = 384
    core = lax.axis_index("core")
    chip = lax.axis_index("y") * 4 + lax.axis_index("width")
    place = jnp.stack([chip, core]).astype(jnp.int32)
    swap = [(0, 1), (1, 0)]
    shape = jax.ShapeDtypeStruct
    with jax.named_scope("earlier_frames"):
        cells = latent.reshape(64, channels)
        before = lax.ppermute(cells, "tm", [(i, i + 1) for i in range(15)])
    with jax.named_scope("weight_slices"):
        turned = jnp.transpose(conv_weight.reshape(TAPS, channels, GROUP), (0, 2, 1))
        pieces = call(weight_body, shape((16, GROUP, DEPTH), BF16), [SMEM, VMEM])(place, turned)
        mine = lax.all_to_all(pieces, "tm", 0, 0).reshape(channels, DEPTH)
        other_half = lax.ppermute(mine, "core", swap)
    with jax.named_scope("activated"):
        before, pieces = lax.optimization_barrier((before, pieces))
        blocks = call(activate_body, shape((4, 2, 4, GROUP, 128), BF16), [VMEM] * 3)(
            before, cells, norm_gain.reshape(1, channels)
        )
        blocks = lax.all_to_all(blocks.reshape(32, GROUP, 128), ("y", "core", "width"), 0, 0)
        patches = call(
            patch_body,
            shape((2, DEPTH, 1024), BF16),
            [VMEM],
            scratch=[pltpu.VMEM((2, DEPTH, 1024), F32)],
        )(blocks.reshape(8, 4, GROUP, 128))
    with jax.named_scope("own_latent"):
        first = core == 0
        kept = jnp.where(first, cells[:32], cells[32:])
        other = lax.ppermute(jnp.where(first, cells[32:], cells[:32]), "core", swap)
        own = jnp.where(first, jnp.concatenate([kept, other]), jnp.concatenate([other, kept]))
    with jax.named_scope("conv"):
        parts = call(conv_body, shape((16, 64, channels), BF16), [SMEM] + [VMEM] * 3, 700_000_000)(
            place, patches, mine, other_half
        )
        parts = lax.all_to_all(parts, PLANE, 0, 0)
    with jax.named_scope("hidden"):
        hidden, normed = call(
            hidden_body, [shape((64, channels), BF16), shape((16, 64, channels), BF16)], [VMEM] * 3
        )(parts, own, attn_gain.reshape(1, channels))
    with jax.named_scope("keys"):
        gathered = lax.all_to_all(normed, PLANE, 0, 0).reshape(1024, channels)
    with jax.named_scope("query"):
        query = call(query_body, shape((64, channels), BF16), [VMEM] * 2, 40_000_000)(normed, w_qkv)
    with jax.named_scope("attention"):
        half = shape((32, channels), BF16)
        keep, send = call(attend_body, [half, half], [SMEM] + [VMEM] * 5, 200_000_000)(
            place, query, gathered, hidden, w_qkv, w_out
        )
        other = lax.ppermute(send, "core", swap)
        out = jnp.where(first, jnp.concatenate([keep, other]), jnp.concatenate([other, keep]))
    return out.reshape(latent.shape)


def solution(mesh):
    devices = mesh.devices.reshape(16, 4, 2, 4)
    fine = Mesh(devices, ("tm", "y", "core", "width"))
    cells = P("tm", ("y", "core"), "width", None)
    in_specs = (cells, P(), P(None, None, None, None, "tm"), P(), P(), P())
    return jax.shard_map(local, mesh=fine, in_specs=in_specs, out_specs=cells, check_vma=False)
```

```python
import functools

import jax
import jax.numpy as jnp
from jax import lax
from jax.experimental import pallas as pl
from jax.experimental.pallas import tpu as pltpu
from jax.sharding import Mesh, PartitionSpec as P

F32 = jnp.float32
BF16 = jnp.bfloat16
TAPS = 27
GROUP = 24
DEPTH = 768
PLANE = ("y", "width")
VMEM = pl.BlockSpec(memory_space=pltpu.VMEM)
SMEM = pl.BlockSpec(memory_space=pltpu.SMEM)
LIMIT = 24 * 1024 * 1024


def call(body, out, specs, flops=1_000_000, moved=1_000_000, scratch=()):
    many = isinstance(out, (tuple, list))
    return pl.pallas_call(
        body,
        out_shape=out,
        in_specs=specs,
        out_specs=[VMEM] * len(out) if many else VMEM,
        scratch_shapes=list(scratch),
        compiler_params=pltpu.CompilerParams(vmem_limit_bytes=LIMIT),
        cost_estimate=pl.CostEstimate(flops=flops, bytes_accessed=moved, transcendentals=0),
    )


def rms_scale(values, gain):
    mean_sq = jnp.mean(values * values, axis=-1, keepdims=True)
    return values * lax.rsqrt(mean_sq + 1e-06) * gain


def weight_body(place_ref, weight_ref, out_ref):
    start = place_ref[0] * GROUP
    source = lax.broadcasted_iota(jnp.int32, (384, 128), 0)
    target = lax.broadcasted_iota(jnp.int32, (384, 128), 1)
    pick = ((target < GROUP) & (source == start + target)).astype(F32).astype(BF16)
    rows = [weight_ref[tap] for tap in range(TAPS)]
    picked = jnp.dot(jnp.concatenate(rows, axis=0), pick, preferred_element_type=F32)
    lane = lax.broadcasted_iota(jnp.int32, (GROUP, 128), 1)
    tiles = [jnp.zeros((GROUP, 128), F32) for _ in range(DEPTH // 128)]
    for tap in range(TAPS):
        value = picked[tap * GROUP : tap * GROUP + GROUP]
        tile, offset = divmod(tap * GROUP, 128)
        value = pltpu.roll(value, offset, 1) if offset else value
        if offset + GROUP > 128:
            tiles[tile] += jnp.where(lane >= offset, value, 0.0)
            tiles[tile + 1] += jnp.where(lane < offset, value, 0.0)
        else:
            tiles[tile] += value
    out_ref[...] = jnp.concatenate(tiles, axis=1).astype(BF16)


def activate_body(before_ref, now_ref, gain_ref, out_ref):
    gain = gain_ref[...]
    halves = []
    for ref in (before_ref, now_ref):
        scaled = rms_scale(ref[...].astype(F32), gain)
        halves.append(scaled / (1.0 + jnp.exp(-scaled)))
    turned = jnp.concatenate(halves, axis=0).T
    later = pltpu.roll(turned, 96, 1)
    for core, whole in ((0, turned), (1, later)):
        for chip in range(16):
            out_ref[chip // 4, core, chip % 4] = whole[chip * GROUP : chip * GROUP + GROUP].astype(BF16)


def patch_body(cells_ref, out_ref, held_ref):
    source = lax.broadcasted_iota(jnp.int32, (128, 384), 0)
    target = lax.broadcasted_iota(jnp.int32, (128, 384), 1)
    frame, row, col = source // 32, (source // 16) % 2, source % 16
    lane = lax.broadcasted_iota(jnp.int32, (8 * GROUP, 128), 1)
    grid = jnp.zeros((8 * GROUP, 384), F32)
    for width in range(4):
        place = (frame < 3) & (target == frame * 128 + row * 64 + width * 16 + col)
        rows = jnp.concatenate([cells_ref[height, width].astype(F32) for height in range(8)], axis=0)
        grid += jnp.dot(rows.astype(BF16), place.astype(F32).astype(BF16), preferred_element_type=F32)
    blank = jnp.zeros((GROUP, 128), F32)
    for time_tap in range(3):
        still = grid[:, time_tap * 128 : time_tap * 128 + 128]
        left = jnp.where(lane % 64 == 0, 0.0, pltpu.roll(still, 1, 1))
        right = jnp.where(lane % 64 == 63, 0.0, pltpu.roll(still, 127, 1))
        for col_tap, base in enumerate((left, still, right)):
            swapped = pltpu.roll(base, 64, 1)
            above = jnp.concatenate([blank, swapped[:-GROUP]], axis=0)
            below = jnp.concatenate([swapped[GROUP:], blank], axis=0)
            up = jnp.where(lane < 64, above, swapped)
            down = jnp.where(lane < 64, swapped, below)
            for row_tap, value in enumerate((up, base, down)):
                tap = (time_tap * 3 + row_tap) * 3 + col_tap
                for height in range(8):
                    held_ref[
                        tap * GROUP : tap * GROUP + GROUP, height * 128 : height * 128 + 128
                    ] = value[height * GROUP : height * GROUP + GROUP]
    held_ref[TAPS * GROUP :, :] = jnp.zeros((DEPTH - TAPS * GROUP, 1024), F32)
    out_ref[...] = held_ref[...].astype(BF16)


def conv_body(patch_ref, weight_ref, out_ref):
    for part in range(4):
        cut = slice(part * 256, part * 256 + 256)
        turned = jnp.dot(weight_ref[...], patch_ref[:, cut], preferred_element_type=F32)
        summed = turned.T.astype(BF16)
        for row in range(4):
            for width in range(4):
                out_ref[part * 4 + width, row * 16 : row * 16 + 16, :] = summed[
                    row * 64 + width * 16 : row * 64 + width * 16 + 16
                ]


def hidden_body(part_ref, latent_ref, gain_ref, hidden_ref, normed_ref):
    summed = latent_ref[...].astype(F32)
    for source in range(16):
        summed += part_ref[source].astype(F32)
    hidden = summed.astype(BF16)
    hidden_ref[...] = hidden
    normed = rms_scale(hidden.astype(F32), gain_ref[...]).astype(BF16)
    for target in range(16):
        normed_ref[target] = normed


def query_body(normed_ref, w_ref, out_ref):
    query = jnp.dot(normed_ref[0], w_ref[:, :384], preferred_element_type=F32).astype(BF16)
    out_ref[...] = lax.dot_general(
        query, w_ref[:, 384:768], (((1,), (1,)), ((), ())), preferred_element_type=F32
    ).astype(BF16)


def attend_body(place_ref, query_ref, cells_ref, hidden_ref, w_ref, w_out_ref, keep_ref, send_ref):
    cells = cells_ref[...]
    scores = lax.dot_general(
        query_ref[...], cells, (((1,), (1,)), ((), ())), preferred_element_type=F32
    ) * (1.0 / 384.0**0.5)
    powers = jnp.exp(scores - jnp.max(scores, axis=-1, keepdims=True))
    total = jnp.sum(powers, axis=-1, keepdims=True)
    mixed = jnp.dot(powers.astype(BF16), cells, preferred_element_type=F32) / total
    attended = jnp.dot(mixed.astype(BF16), w_ref[:, 768:], preferred_element_type=F32)
    update = jnp.dot(attended.astype(BF16), w_out_ref[...], preferred_element_type=F32)
    decoded = (hidden_ref[...].astype(F32) + update).astype(BF16)
    first = place_ref[1] == 0
    keep_ref[...] = jnp.where(first, decoded[:32], decoded[32:])
    send_ref[...] = jnp.where(first, decoded[32:], decoded[:32])


def local(latent, norm_gain, conv_weight, attn_gain, w_qkv, w_out):
    channels = 384
    core = lax.axis_index("core")
    chip = lax.axis_index("y") * 4 + lax.axis_index("width")
    place = jnp.stack([chip, core]).astype(jnp.int32)
    swap = [(0, 1), (1, 0)]
    shape = jax.ShapeDtypeStruct
    with jax.named_scope("earlier_frames"):
        cells = latent.reshape(64, channels)
        before = lax.ppermute(cells, "tm", [(i, i + 1) for i in range(15)])
    with jax.named_scope("weight_slices"):
        turned = jnp.transpose(conv_weight.reshape(TAPS, channels, GROUP), (0, 2, 1))
        piece = call(weight_body, shape((GROUP, DEPTH), BF16), [SMEM, VMEM])(place, turned)
    with jax.named_scope("activated"):
        blocks = call(activate_body, shape((4, 2, 4, GROUP, 128), BF16), [VMEM] * 3)(
            before, cells, norm_gain.reshape(1, channels)
        )
        piece, blocks = lax.optimization_barrier((piece, blocks))
        weight = lax.all_gather(piece, "tm", axis=0, tiled=True)
        blocks = lax.all_to_all(blocks.reshape(32, GROUP, 128), ("y", "core", "width"), 0, 0)
        patches = call(
            patch_body,
            shape((DEPTH, 1024), BF16),
            [VMEM],
            scratch=[pltpu.VMEM((DEPTH, 1024), F32)],
        )(blocks.reshape(8, 4, GROUP, 128))
    with jax.named_scope("own_latent"):
        first = core == 0
        kept = jnp.where(first, cells[:32], cells[32:])
        other = lax.ppermute(jnp.where(first, cells[32:], cells[:32]), "core", swap)
        own = jnp.where(first, jnp.concatenate([kept, other]), jnp.concatenate([other, kept]))
    with jax.named_scope("conv"):
        parts = call(conv_body, shape((16, 64, channels), BF16), [VMEM] * 2, 700_000_000)(patches, weight)
        parts = lax.all_to_all(parts, PLANE, 0, 0)
    with jax.named_scope("hidden"):
        hidden, normed = call(
            hidden_body, [shape((64, channels), BF16), shape((16, 64, channels), BF16)], [VMEM] * 3
        )(parts, own, attn_gain.reshape(1, channels))
    with jax.named_scope("keys"):
        gathered = lax.all_to_all(normed, PLANE, 0, 0).reshape(1024, channels)
    with jax.named_scope("query"):
        query = call(query_body, shape((64, channels), BF16), [VMEM] * 2, 40_000_000)(normed, w_qkv)
    with jax.named_scope("attention"):
        half = shape((32, channels), BF16)
        keep, send = call(attend_body, [half, half], [SMEM] + [VMEM] * 5, 200_000_000)(
            place, query, gathered, hidden, w_qkv, w_out
        )
        other = lax.ppermute(send, "core", swap)
        out = jnp.where(first, jnp.concatenate([keep, other]), jnp.concatenate([other, keep]))
    return out.reshape(latent.shape)


def solution(mesh):
    devices = mesh.devices.reshape(16, 4, 2, 4)
    fine = Mesh(devices, ("tm", "y", "core", "width"))
    cells = P("tm", ("y", "core"), "width", None)
    in_specs = (cells, P(), P(None, None, None, None, "tm"), P(), P(), P())
    return jax.shard_map(local, mesh=fine, in_specs=in_specs, out_specs=cells, check_vma=False)
```

```python
import functools

import jax
import jax.numpy as jnp
from jax import lax
from jax.experimental import pallas as pl
from jax.experimental.pallas import tpu as pltpu
from jax.sharding import Mesh, PartitionSpec as P

F32 = jnp.float32
BF16 = jnp.bfloat16
TAPS = 27
GROUP = 24
SLOT = 96
DEPTH = 2688
PLANE = ("y", "width")
VMEM = pl.BlockSpec(memory_space=pltpu.VMEM)
SMEM = pl.BlockSpec(memory_space=pltpu.SMEM)
LIMIT = 32 * 1024 * 1024


def call(body, out, specs, flops=1_000_000, moved=1_000_000, scratch=()):
    many = isinstance(out, (tuple, list))
    return pl.pallas_call(
        body,
        out_shape=out,
        in_specs=specs,
        out_specs=[VMEM] * len(out) if many else VMEM,
        scratch_shapes=list(scratch),
        compiler_params=pltpu.CompilerParams(vmem_limit_bytes=LIMIT),
        cost_estimate=pl.CostEstimate(flops=flops, bytes_accessed=moved, transcendentals=0),
    )


def one_hot(shape, match):
    row = lax.broadcasted_iota(jnp.int32, shape, 0)
    col = lax.broadcasted_iota(jnp.int32, shape, 1)
    return match(row, col).astype(F32).astype(BF16)


def channel_of(place):
    return place % SLOT // 6 * GROUP + place // SLOT * 6 + place % 6


def weight_body(place_ref, weight_ref, out_ref):
    start = place_ref[3] * SLOT
    pick = one_hot((384, 128), lambda source, target: (target < SLOT) & (source == start + target))
    rows = jnp.concatenate([weight_ref[tap] for tap in range(TAPS)], axis=0)
    picked = jnp.dot(rows, pick, preferred_element_type=F32)
    upper = place_ref[1] // 2
    picked = jnp.where(upper == 0, picked, pltpu.roll(picked, TAPS * GROUP - 12, 0))
    picked = jnp.where(place_ref[1] % 2 == 0, picked, pltpu.roll(picked, TAPS * GROUP - 6, 0))
    lane = lax.broadcasted_iota(jnp.int32, (8, 128), 1)
    kept = lax.broadcasted_iota(jnp.int32, (8, 128), 0) < 6
    tiles = [jnp.zeros((8, 128), F32) for _ in range(DEPTH // 128)]
    for tap in range(TAPS):
        value = jnp.where(kept, picked[tap * GROUP : tap * GROUP + 8], 0.0)
        tile, offset = divmod(tap * SLOT, 128)
        value = pltpu.roll(value, offset, 1) if offset else value
        if offset + SLOT > 128:
            tiles[tile] += jnp.where(lane >= offset, value, 0.0)
            tiles[tile + 1] += jnp.where(lane < offset, value, 0.0)
        else:
            tiles[tile] += value
    out_ref[...] = jnp.concatenate(tiles, axis=1).astype(BF16)


def activate_body(before_ref, now_ref, gain_ref, out_ref):
    gain = gain_ref[...]
    halves = []
    for ref in (before_ref, now_ref):
        scaled = rms_scale(ref[...].astype(F32), gain)
        halves.append(scaled / (1.0 + jnp.exp(-scaled)))
    turned = jnp.concatenate(halves, axis=0).T
    later = pltpu.roll(turned, 96, 1)
    now = now_ref[...]
    order = one_hot((384, 384), lambda place, source: source == channel_of(place))
    latent = lax.dot_general(
        order, jnp.concatenate([now, now], axis=0), (((1,), (1,)), ((), ())), preferred_element_type=F32
    )
    lane = lax.broadcasted_iota(jnp.int32, (GROUP, 128), 1)
    for row in range(4):
        for core in range(2):
            packed = jnp.zeros((GROUP, 128), F32)
            for member in range(4):
                part = latent[row * SLOT + member * GROUP : row * SLOT + member * GROUP + GROUP]
                shift = (32 * member - 32 * core) % 128
                part = pltpu.roll(part, shift, 1) if shift else part
                packed += jnp.where((lane >= 32 * member) & (lane < 32 * member + 32), part, 0.0)
            packed = packed.astype(BF16)
            whole = (later if core else turned).astype(BF16)
            for width in range(4):
                out_ref[row, core, width, :SLOT, :] = whole[width * SLOT : width * SLOT + SLOT]
                out_ref[row, core, width, SLOT:, :] = packed


def patch_body(place_ref, cells_ref, out_ref, latent_ref):
    source = lax.broadcasted_iota(jnp.int32, (128, 384), 0)
    target = lax.broadcasted_iota(jnp.int32, (128, 384), 1)
    frame, row, col = source // 32, (source // 16) % 2, source % 16
    lane = lax.broadcasted_iota(jnp.int32, (8 * SLOT, 128), 1)
    grid = jnp.zeros((8 * SLOT, 384), F32)
    for width in range(4):
        place = (frame < 3) & (target == frame * 128 + row * 64 + width * 16 + col)
        rows = jnp.concatenate([cells_ref[height, width, :SLOT, :] for height in range(8)], axis=0)
        grid += jnp.dot(rows, place.astype(F32).astype(BF16), preferred_element_type=F32)
    blank = jnp.zeros((SLOT, 128), F32)
    for time_tap in range(3):
        still = grid[:, time_tap * 128 : time_tap * 128 + 128]
        left = jnp.where(lane % 64 == 0, 0.0, pltpu.roll(still, 1, 1))
        right = jnp.where(lane % 64 == 63, 0.0, pltpu.roll(still, 127, 1))
        for col_tap, base in enumerate((left, still, right)):
            swapped = pltpu.roll(base, 64, 1)
            above = jnp.concatenate([blank, swapped[:-SLOT]], axis=0)
            below = jnp.concatenate([swapped[SLOT:], blank], axis=0)
            up = jnp.where(lane < 64, above, swapped)
            down = jnp.where(lane < 64, swapped, below)
            for row_tap, value in enumerate((up, base, down)):
                tap = (time_tap * 3 + row_tap) * 3 + col_tap
                value = value.astype(BF16)
                for height in range(8):
                    out_ref[tap * SLOT : tap * SLOT + SLOT, height * 128 : height * 128 + 128] = value[
                        height * SLOT : height * SLOT + SLOT
                    ]
    out_ref[TAPS * SLOT :, :] = jnp.zeros((DEPTH - TAPS * SLOT, 1024), BF16)
    lane = lax.broadcasted_iota(jnp.int32, (GROUP, 128), 1)
    for member in range(4):
        for tile in range(2):
            packed = jnp.zeros((GROUP, 128), F32)
            for height in range(4):
                part = cells_ref[tile * 4 + height, place_ref[3]].astype(F32)[SLOT:]
                shift = (32 * height - 32 * member) % 128
                part = pltpu.roll(part, shift, 1) if shift else part
                packed += jnp.where((lane >= 32 * height) & (lane < 32 * height + 32), part, 0.0)
            latent_ref[member * GROUP : member * GROUP + GROUP, tile * 128 : tile * 128 + 128] = packed


def conv_body(patch_ref, weight_ref, out_ref):
    dense = one_hot((SLOT, 128), lambda row, col: col == row // 6 * 8 + row % 6)
    weight = jnp.dot(dense, weight_ref[...], preferred_element_type=F32).astype(BF16)
    pieces = []
    for part in range(4):
        cut = slice(part * 256, part * 256 + 256)
        pieces.append(jnp.dot(weight, patch_ref[:, cut], preferred_element_type=F32).T)
    for width in range(4):
        rows = [
            pieces[row // 4][row % 4 * 64 + width * 16 : row % 4 * 64 + width * 16 + 16] for row in range(16)
        ]
        out_ref[width] = jnp.concatenate(rows, axis=0).T.astype(BF16)


def hidden_body(part_ref, latent_ref, out_ref):
    summed = latent_ref[...]
    for source in range(4):
        summed += part_ref[source].astype(F32)
    hidden = summed.astype(BF16)
    for target in range(16):
        out_ref[target] = hidden


def column_scale(values, gain):
    mean_sq = jnp.mean(values * values, axis=0, keepdims=True)
    return values * lax.rsqrt(mean_sq + 1e-06) * gain


def attend_body(place_ref, block_ref, gain_ref, w_ref, w_out_ref, keep_ref, send_ref, hidden_ref):
    for row in range(4):
        for width in range(4):
            hidden_ref[row * SLOT : row * SLOT + SLOT, width * 256 : width * 256 + 256] = block_ref[
                row * 4 + width
            ].astype(F32)
    gain = gain_ref[...]
    cells = column_scale(hidden_ref[...], gain).astype(BF16)
    own_start = pl.multiple_of(place_ref[3] * 256 + place_ref[1] // 2 * 128, 128)
    own = hidden_ref[:, pl.ds(own_start, 128)]
    own_normed = column_scale(own, gain).T
    own = own.T
    upper = place_ref[1] % 2 == 0
    order = one_hot((384, 384), lambda place, source: source == channel_of(place))
    hidden = jnp.where(upper, own[:64], own[64:]).astype(BF16)
    normed = jnp.where(upper, own_normed[:64], own_normed[64:]).astype(BF16)
    both = jnp.concatenate([hidden, normed], axis=0)
    both = jnp.dot(both, order, preferred_element_type=F32)
    hidden, normed = both[:64], both[64:].astype(BF16)
    query = jnp.dot(normed, w_ref[:, :384], preferred_element_type=F32).astype(BF16)
    query = lax.dot_general(
        query, w_ref[:, 384:768], (((1,), (1,)), ((), ())), preferred_element_type=F32
    ).astype(BF16)
    query = lax.dot_general(
        query, order, (((1,), (1,)), ((), ())), preferred_element_type=F32
    ).astype(BF16)
    scores = jnp.dot(query, cells, preferred_element_type=F32) * (1.0 / 384.0**0.5)
    powers = jnp.exp(scores - jnp.max(scores, axis=-1, keepdims=True))
    total = jnp.sum(powers, axis=-1, keepdims=True)
    mixed = lax.dot_general(
        powers.astype(BF16), cells, (((1,), (1,)), ((), ())), preferred_element_type=F32
    )
    mixed = jnp.dot((mixed / total).astype(BF16), order, preferred_element_type=F32).astype(BF16)
    attended = jnp.dot(mixed, w_ref[:, 768:], preferred_element_type=F32).astype(BF16)
    update = jnp.dot(attended, w_out_ref[...], preferred_element_type=F32)
    decoded = (hidden + update).astype(BF16)
    first = place_ref[2] == 0
    keep_ref[...] = jnp.where(first, decoded[:32], decoded[32:])
    send_ref[...] = jnp.where(first, decoded[32:], decoded[:32])


def rms_scale(values, gain):
    mean_sq = jnp.mean(values * values, axis=-1, keepdims=True)
    return values * lax.rsqrt(mean_sq + 1e-06) * gain


def local(latent, norm_gain, conv_weight, attn_gain, w_qkv, w_out):
    channels = 384
    core = lax.axis_index("core")
    place = [lax.axis_index("tm"), lax.axis_index("y"), core, lax.axis_index("width")]
    place = jnp.stack(place).astype(jnp.int32)
    swap = [(0, 1), (1, 0)]
    shape = jax.ShapeDtypeStruct
    with jax.named_scope("earlier_frames"):
        cells = latent.reshape(64, channels)
        before = lax.ppermute(cells, "tm", [(i, i + 1) for i in range(15)])
    with jax.named_scope("weight_slices"):
        turned = jnp.transpose(conv_weight.reshape(TAPS, channels, GROUP), (0, 2, 1))
        piece = call(weight_body, shape((8, DEPTH), BF16), [SMEM, VMEM])(place, turned)
    with jax.named_scope("activated"):
        blocks = call(activate_body, shape((4, 2, 4, SLOT + GROUP, 128), BF16), [VMEM] * 3)(
            before, cells, norm_gain.reshape(1, channels)
        )
        piece, blocks = lax.optimization_barrier((piece, blocks))
        weight = lax.all_gather(piece, "tm", axis=0, tiled=True)
        blocks = lax.all_to_all(blocks.reshape(32, SLOT + GROUP, 128), ("y", "core", "width"), 0, 0)
        patches, own = call(
            patch_body, [shape((DEPTH, 1024), BF16), shape((SLOT, 256), F32)], [SMEM, VMEM]
        )(place, blocks.reshape(8, 4, SLOT + GROUP, 128))
    with jax.named_scope("conv"):
        parts = call(conv_body, shape((4, SLOT, 256), BF16), [VMEM] * 2, 700_000_000)(patches, weight)
        parts = lax.all_to_all(parts, "width", 0, 0)
    with jax.named_scope("hidden"):
        hidden = call(hidden_body, shape((16, SLOT, 256), BF16), [VMEM] * 2)(parts, own)
        hidden = lax.all_to_all(hidden, PLANE, 0, 0)
    with jax.named_scope("attention"):
        gain = attn_gain.reshape(16, 4, 6).transpose(1, 0, 2).reshape(channels, 1)
        half = shape((32, channels), BF16)
        keep, send = call(
            attend_body,
            [half, half],
            [SMEM] + [VMEM] * 4,
            200_000_000,
            scratch=[pltpu.VMEM((channels, 1024), F32)],
        )(place, hidden, gain, w_qkv, w_out)
        got = lax.ppermute(send, "core", swap)
        out = jnp.where(core == 0, jnp.concatenate([keep, got]), jnp.concatenate([got, keep]))
    return out.reshape(latent.shape)


def solution(mesh):
    devices = mesh.devices.reshape(16, 4, 2, 4)
    fine = Mesh(devices, ("tm", "y", "core", "width"))
    cells = P("tm", ("y", "core"), "width", None)
    in_specs = (cells, P(), P(None, None, None, None, "tm"), P(), P(), P())
    return jax.shard_map(local, mesh=fine, in_specs=in_specs, out_specs=cells, check_vma=False)
```

```python
import functools

import jax
import jax.numpy as jnp
from jax import lax
from jax.experimental import pallas as pl
from jax.experimental.pallas import tpu as pltpu
from jax.sharding import Mesh, PartitionSpec as P

F32 = jnp.float32
BF16 = jnp.bfloat16
TAPS = 27
GROUP = 24
SLOT = 96
BAND = 896
PLANE = ("width", "y")
VMEM = pl.BlockSpec(memory_space=pltpu.VMEM)
SMEM = pl.BlockSpec(memory_space=pltpu.SMEM)
HBM = pl.BlockSpec(memory_space=pltpu.HBM)
LIMIT = 12 * 1024 * 1024
FIRST_LIMIT = 54784 * 1024


def call(body, out, specs, flops=1_000_000, moved=1_000_000, scratch=(), limit=LIMIT):
    many = isinstance(out, (tuple, list))
    return pl.pallas_call(
        body,
        out_shape=out,
        in_specs=specs,
        out_specs=[VMEM] * len(out) if many else VMEM,
        scratch_shapes=list(scratch),
        compiler_params=pltpu.CompilerParams(vmem_limit_bytes=limit),
        cost_estimate=pl.CostEstimate(flops=flops, bytes_accessed=moved, transcendentals=0),
    )


def one_hot(shape, column_of):
    row = lax.broadcasted_iota(jnp.int32, (shape[0], 1), 0)
    col = lax.broadcasted_iota(jnp.int32, shape, 1)
    return (col == column_of(row)).astype(F32).astype(BF16)


def channel_of(place):
    return place % SLOT // 6 * GROUP + place // SLOT * 6 + place % 6


def activated(values, gain):
    scaled = rms_scale(values.astype(F32), gain)
    return scaled / (1.0 + jnp.exp(-scaled))


def first_body(place_ref, weight_hbm, latent_hbm, gain_ref, piece_ref, own_ref, pack_ref, weight_ref, latent_ref, sems):
    weight_copy = pltpu.make_async_copy(weight_hbm, weight_ref, sems.at[0])
    latent_copy = pltpu.make_async_copy(latent_hbm, latent_ref, sems.at[1])
    weight_copy.start()
    latent_copy.start()
    start = place_ref[3] * SLOT
    pick = one_hot((384, 128), lambda row: jnp.where(row - start < SLOT, row - start, -1))
    order = one_hot((384, 384), channel_of)
    latent_copy.wait()
    now = latent_ref[...]
    own_ref[...] = activated(now, gain_ref[...])
    latent = lax.dot_general(
        order, jnp.concatenate([now, now], axis=0), (((1,), (1,)), ((), ())), preferred_element_type=F32
    )
    lane = lax.broadcasted_iota(jnp.int32, (GROUP, 128), 1)
    for row in range(4):
        for core in range(2):
            packed = jnp.zeros((GROUP, 128), F32)
            for member in range(4):
                part = latent[row * SLOT + member * GROUP : row * SLOT + member * GROUP + GROUP]
                shift = (32 * member - 32 * core) % 128
                part = pltpu.roll(part, shift, 1) if shift else part
                packed += jnp.where((lane >= 32 * member) & (lane < 32 * member + 32), part, 0.0)
            pack_ref[row, core] = packed.astype(BF16)
    weight_copy.wait()
    rows = jnp.concatenate([weight_ref[tap] for tap in range(TAPS)], axis=0)
    picked = jnp.dot(rows, pick, preferred_element_type=F32)
    upper = place_ref[1] // 2
    picked = jnp.where(upper == 0, picked, pltpu.roll(picked, TAPS * GROUP - 12, 0))
    picked = jnp.where(place_ref[1] % 2 == 0, picked, pltpu.roll(picked, TAPS * GROUP - 6, 0))
    lane = lax.broadcasted_iota(jnp.int32, (8, 128), 1)
    kept = lax.broadcasted_iota(jnp.int32, (8, 128), 0) < 6
    tiles = [jnp.zeros((8, 128), F32) for _ in range(3 * BAND // 128)]
    for row_tap in range(3):
        for slot in range(9):
            tap = slot // 3 * 9 + row_tap * 3 + slot % 3
            value = jnp.where(kept, picked[tap * GROUP : tap * GROUP + 8], 0.0)
            tile, offset = divmod(row_tap * BAND + slot * SLOT, 128)
            value = pltpu.roll(value, offset, 1) if offset else value
            if offset + SLOT > 128:
                tiles[tile] += jnp.where(lane >= offset, value, 0.0)
                tiles[tile + 1] += jnp.where(lane < offset, value, 0.0)
            else:
                tiles[tile] += value
    main, spare = [], [[], []]
    for tile in range(BAND // 128):
        stack = jnp.concatenate([tiles[band * 7 + tile][:6] for band in range(3)], axis=0)
        main.append(stack[:16])
        spare[0].append(stack[16:17])
        spare[1].append(stack[17:])
    spare = jnp.concatenate(spare[0] + spare[1] + [jnp.zeros((2, 128), F32)], axis=0)
    piece_ref[...] = jnp.concatenate(main + [spare], axis=1).astype(BF16)


def block_body(before_ref, own_ref, pack_ref, gain_ref, out_ref):
    early = activated(before_ref[...], gain_ref[...])
    turned = jnp.concatenate([early, own_ref[...]], axis=0).T
    later = pltpu.roll(turned, 96, 1).astype(BF16)
    turned = turned.astype(BF16)
    for row in range(4):
        for core in range(2):
            whole = later if core else turned
            for width in range(4):
                out_ref[width, row, core, :SLOT, :] = whole[width * SLOT : width * SLOT + SLOT]
                out_ref[width, row, core, SLOT:, :] = pack_ref[row, core]


def grid_place(row):
    frame = row // 32 % 4
    target = frame * 128 + row // 16 % 2 * 64 + row // 128 * 16 + row % 16
    return jnp.where(frame < 3, target, -1)


def main_place(row):
    part = row // SLOT * 6 + row % 6
    return jnp.where(part < 16, row % SLOT // 6 * 16 + part, -1)


def spare_place(tile, row):
    part = row % 6 - 4
    return jnp.where(part >= 0, row // 6 * 16 + part * 7 + tile, -1)


def conv_body(place_ref, cells_ref, weight_ref, out_ref, latent_ref, flat_ref):
    lane = lax.broadcasted_iota(jnp.int32, (8 * SLOT, 128), 1) % 64
    rows = [
        jnp.concatenate([cells_ref[width, height, :SLOT, :] for height in range(8)], axis=0)
        for width in range(4)
    ]
    grid = jnp.dot(
        jnp.concatenate(rows, axis=1), one_hot((512, 384), grid_place), preferred_element_type=F32
    )
    for time_tap in range(3):
        still = grid[:, time_tap * 128 : time_tap * 128 + 128]
        left = jnp.where(lane == 0, 0.0, pltpu.roll(still, 1, 1))
        right = jnp.where(lane == 63, 0.0, pltpu.roll(still, 127, 1))
        for col_tap, base in enumerate((left, still, right)):
            slot = (time_tap * 3 + col_tap) * SLOT
            base = base.astype(BF16)
            for height in range(8):
                flat_ref[slot : slot + SLOT, height * 128 : height * 128 + 128] = base[
                    height * SLOT : height * SLOT + SLOT
                ]
    flat_ref[9 * SLOT :, :] = jnp.zeros((BAND - 9 * SLOT, 1024), BF16)
    main = jnp.dot(one_hot((3 * SLOT, 256), main_place), weight_ref[:, :BAND], preferred_element_type=F32)
    spare = [
        jnp.dot(
            one_hot((SLOT, 256), functools.partial(spare_place, tile)),
            weight_ref[:, BAND:],
            preferred_element_type=F32,
        )
        for tile in range(BAND // 128)
    ]
    last = main[2 * SLOT :] + jnp.concatenate(spare, axis=1)
    weight = jnp.concatenate([main[: 2 * SLOT], last], axis=0).astype(BF16)
    whole = jnp.dot(weight, flat_ref[...], preferred_element_type=F32)
    lane = lax.broadcasted_iota(jnp.int32, (SLOT, 1024), 1)
    total = whole[SLOT : 2 * SLOT]
    total += jnp.where(lane < 64, 0.0, pltpu.roll(whole[:SLOT], 64, 1))
    total += jnp.where(lane < 960, pltpu.roll(whole[2 * SLOT :], 960, 1), 0.0)
    pieces = [total[:, part * 256 : part * 256 + 256].T for part in range(4)]
    for width in range(4):
        rows = [
            pieces[row // 4][row % 4 * 64 + width * 16 : row % 4 * 64 + width * 16 + 16] for row in range(16)
        ]
        out_ref[width] = jnp.concatenate(rows, axis=0).T.astype(BF16)
    lane = lax.broadcasted_iota(jnp.int32, (GROUP, 128), 1)
    for member in range(4):
        for tile in range(2):
            packed = jnp.zeros((GROUP, 128), F32)
            for height in range(4):
                part = cells_ref[place_ref[3], tile * 4 + height].astype(F32)[SLOT:]
                shift = (32 * height - 32 * member) % 128
                part = pltpu.roll(part, shift, 1) if shift else part
                packed += jnp.where((lane >= 32 * height) & (lane < 32 * height + 32), part, 0.0)
            latent_ref[member * GROUP : member * GROUP + GROUP, tile * 128 : tile * 128 + 128] = packed


def hidden_body(part_ref, latent_ref, out_ref):
    summed = latent_ref[...]
    for source in range(4):
        summed += part_ref[source].astype(F32)
    hidden = summed.astype(BF16)
    for target in range(16):
        out_ref[target] = hidden


def column_scale(values, gain):
    mean_sq = jnp.mean(values * values, axis=0, keepdims=True)
    return values * lax.rsqrt(mean_sq + 1e-06) * gain


def fold_body(w_ref, w_out_ref, score_ref, update_ref):
    order = one_hot((384, 384), channel_of)
    turned = jnp.dot(order, w_ref[...], preferred_element_type=F32).astype(BF16)
    score = lax.dot_general(
        turned[:, :384], turned[:, 384:768], (((1,), (1,)), ((), ())), preferred_element_type=F32
    )
    score_ref[...] = (score * (1.0 / 384.0**0.5)).astype(BF16)
    update_ref[...] = jnp.dot(turned[:, 768:], w_out_ref[...], preferred_element_type=F32).astype(BF16)


def attend_body(place_ref, block_ref, gain_ref, score_ref, update_ref, keep_ref, send_ref, hidden_ref, cells_ref):
    for row in range(4):
        for width in range(4):
            hidden_ref[row * SLOT : row * SLOT + SLOT, width * 256 : width * 256 + 256] = block_ref[
                width * 4 + row
            ].astype(F32)
    cells = column_scale(hidden_ref[...], gain_ref[...]).astype(BF16)
    cells_ref[...] = cells
    own_cut = pl.ds(pl.multiple_of(place_ref[3] * 256 + place_ref[1] // 2 * 128, 128), 128)
    upper = place_ref[1] % 2 == 0
    own_normed = cells_ref[:, own_cut].astype(F32).T
    own_normed = jnp.where(upper, own_normed[:64], own_normed[64:]).astype(BF16)
    own = hidden_ref[:, own_cut].T
    own = jnp.where(upper, own[:64], own[64:]).astype(BF16)
    order = one_hot((384, 384), channel_of)
    own = jnp.dot(own, order, preferred_element_type=F32)
    query = jnp.dot(own_normed, score_ref[...], preferred_element_type=F32).astype(BF16)
    scores = jnp.dot(query, cells, preferred_element_type=F32)
    powers = jnp.exp(scores - jnp.max(scores, axis=-1, keepdims=True))
    total = jnp.sum(powers, axis=-1, keepdims=True)
    mixed = lax.dot_general(
        powers.astype(BF16), cells, (((1,), (1,)), ((), ())), preferred_element_type=F32
    )
    mixed = (mixed / total).astype(BF16)
    decoded = (own + jnp.dot(mixed, update_ref[...], preferred_element_type=F32)).astype(BF16)
    first = place_ref[2] == 0
    keep_ref[...] = jnp.where(first, decoded[:32], decoded[32:])
    send_ref[...] = jnp.where(first, decoded[32:], decoded[:32])


def rms_scale(values, gain):
    mean_sq = jnp.mean(values * values, axis=-1, keepdims=True)
    return values * lax.rsqrt(mean_sq + 1e-06) * gain


def local(latent, norm_gain, conv_weight, attn_gain, w_qkv, w_out):
    channels = 384
    core = lax.axis_index("core")
    place = [lax.axis_index("tm"), lax.axis_index("y"), core, lax.axis_index("width")]
    place = jnp.stack(place).astype(jnp.int32)
    swap = [(0, 1), (1, 0)]
    shape = jax.ShapeDtypeStruct
    with jax.named_scope("earlier_frames"):
        cells = latent.reshape(64, channels)
        before = lax.ppermute(cells, "tm", [(i, i + 1) for i in range(15)])
    with jax.named_scope("activated"):
        gain = norm_gain.reshape(1, channels)
        turned = jnp.transpose(conv_weight.reshape(TAPS, channels, GROUP), (0, 2, 1))
        piece, now, pack = call(
            first_body,
            [shape((16, 1024), BF16), shape((64, channels), F32), shape((4, 2, GROUP, 128), BF16)],
            [SMEM, HBM, HBM, VMEM],
            scratch=[
                pltpu.VMEM((TAPS, GROUP, channels), BF16),
                pltpu.VMEM((64, channels), BF16),
                pltpu.SemaphoreType.DMA((2,)),
            ],
            limit=FIRST_LIMIT,
        )(place, turned, cells, gain)
        blocks = call(block_body, shape((4, 4, 2, SLOT + GROUP, 128), BF16), [VMEM] * 4)(
            before, now, pack, gain
        )
        piece, blocks = lax.optimization_barrier((piece, blocks))
        weight = lax.all_gather(piece, "tm", axis=0, tiled=True)
        blocks = lax.all_to_all(blocks.reshape(32, SLOT + GROUP, 128), ("width", "y", "core"), 0, 0)
    with jax.named_scope("conv"):
        parts, own = call(
            conv_body,
            [shape((4, SLOT, 256), BF16), shape((SLOT, 256), F32)],
            [SMEM, VMEM, VMEM],
            700_000_000,
            scratch=[pltpu.VMEM((BAND, 1024), BF16)],
        )(place, blocks.reshape(4, 8, SLOT + GROUP, 128), weight)
        parts = lax.all_to_all(parts, "width", 0, 0)
    with jax.named_scope("hidden"):
        hidden = call(hidden_body, shape((16, SLOT, 256), BF16), [VMEM] * 2)(parts, own)
        hidden = lax.all_to_all(hidden, PLANE, 0, 0)
    with jax.named_scope("attention"):
        gain = attn_gain.reshape(16, 4, 6).transpose(1, 0, 2).reshape(channels, 1)
        square, half = shape((channels, channels), BF16), shape((32, channels), BF16)
        score, update = call(fold_body, [square, square], [VMEM] * 2, 600_000_000)(w_qkv, w_out)
        keep, send = call(
            attend_body,
            [half, half],
            [SMEM] + [VMEM] * 4,
            200_000_000,
            scratch=[pltpu.VMEM((channels, 1024), F32), pltpu.VMEM((channels, 1024), BF16)],
        )(place, hidden, gain, score, update)
        got = lax.ppermute(send, "core", swap)
        out = jnp.where(core == 0, jnp.concatenate([keep, got]), jnp.concatenate([got, keep]))
    return out.reshape(latent.shape)


def solution(mesh):
    devices = mesh.devices.reshape(16, 4, 2, 4)
    fine = Mesh(devices, ("tm", "y", "core", "width"))
    cells = P("tm", ("y", "core"), "width", None)
    in_specs = (cells, P(), P(None, None, None, None, "tm"), P(), P(), P())
    return jax.shard_map(local, mesh=fine, in_specs=in_specs, out_specs=cells, check_vma=False)
```

```python
import functools

import jax
import jax.numpy as jnp
from jax import lax
from jax.experimental import pallas as pl
from jax.experimental.pallas import tpu as pltpu
from jax.sharding import Mesh, PartitionSpec as P

F32 = jnp.float32
BF16 = jnp.bfloat16
TAPS = 27
GROUP = 24
SLOT = 96
BAND = 896
PLANE = ("width", "y")
VMEM = pl.BlockSpec(memory_space=pltpu.VMEM)
SMEM = pl.BlockSpec(memory_space=pltpu.SMEM)
HBM = pl.BlockSpec(memory_space=pltpu.HBM)
LIMIT = 12 * 1024 * 1024
FIRST_LIMIT = 55072 * 1024


def call(body, out, specs, flops=1_000_000, moved=1_000_000, scratch=(), limit=LIMIT):
    many = isinstance(out, (tuple, list))
    return pl.pallas_call(
        body,
        out_shape=out,
        in_specs=specs,
        out_specs=[VMEM] * len(out) if many else VMEM,
        scratch_shapes=list(scratch),
        compiler_params=pltpu.CompilerParams(vmem_limit_bytes=limit),
        cost_estimate=pl.CostEstimate(flops=flops, bytes_accessed=moved, transcendentals=0),
    )


def one_hot(shape, column_of):
    row = lax.broadcasted_iota(jnp.int32, (shape[0], 1), 0)
    col = lax.broadcasted_iota(jnp.int32, shape, 1)
    return (col == column_of(row)).astype(F32).astype(BF16)


def channel_of(place):
    return place % SLOT // 6 * GROUP + place // SLOT * 6 + place % 6


def activated(values, gain):
    scaled = rms_scale(values.astype(F32), gain)
    return scaled / (1.0 + jnp.exp(-scaled))


def first_body(
    place_ref, weight_hbm, latent_hbm, gain_hbm, piece_ref, own_ref, pack_ref, weight_ref, latent_ref, gain_ref, sems
):
    weight_copy = pltpu.make_async_copy(weight_hbm, weight_ref, sems.at[0])
    latent_copy = pltpu.make_async_copy(latent_hbm, latent_ref, sems.at[1])
    gain_copy = pltpu.make_async_copy(gain_hbm, gain_ref, sems.at[2])
    latent_copy.start()
    gain_copy.start()
    weight_copy.start()
    start = place_ref[3] * SLOT
    pick = one_hot((384, 128), lambda row: jnp.where(row - start < SLOT, row - start, -1))
    order = one_hot((384, 384), channel_of)
    latent_copy.wait()
    gain_copy.wait()
    now = latent_ref[...]
    own_ref[...] = activated(now, gain_ref[...].reshape(1, 384)).astype(BF16)
    latent = lax.dot_general(
        order, jnp.concatenate([now, now], axis=0), (((1,), (1,)), ((), ())), preferred_element_type=F32
    )
    lane = lax.broadcasted_iota(jnp.int32, (GROUP, 128), 1)
    for row in range(4):
        for core in range(2):
            packed = jnp.zeros((GROUP, 128), F32)
            for member in range(4):
                part = latent[row * SLOT + member * GROUP : row * SLOT + member * GROUP + GROUP]
                shift = (32 * member - 32 * core) % 128
                part = pltpu.roll(part, shift, 1) if shift else part
                packed += jnp.where((lane >= 32 * member) & (lane < 32 * member + 32), part, 0.0)
            pack_ref[row, core] = packed.astype(BF16)
    weight_copy.wait()
    rows = jnp.concatenate([weight_ref[tap] for tap in range(TAPS)], axis=0)
    picked = jnp.dot(rows, pick, preferred_element_type=F32)
    upper = place_ref[1] // 2
    picked = jnp.where(upper == 0, picked, pltpu.roll(picked, TAPS * GROUP - 12, 0))
    picked = jnp.where(place_ref[1] % 2 == 0, picked, pltpu.roll(picked, TAPS * GROUP - 6, 0))
    lane = lax.broadcasted_iota(jnp.int32, (8, 128), 1)
    kept = lax.broadcasted_iota(jnp.int32, (8, 128), 0) < 6
    tiles = [jnp.zeros((8, 128), F32) for _ in range(3 * BAND // 128)]
    for row_tap in range(3):
        for slot in range(9):
            tap = slot // 3 * 9 + row_tap * 3 + slot % 3
            value = jnp.where(kept, picked[tap * GROUP : tap * GROUP + 8], 0.0)
            tile, offset = divmod(row_tap * BAND + slot * SLOT, 128)
            value = pltpu.roll(value, offset, 1) if offset else value
            if offset + SLOT > 128:
                tiles[tile] += jnp.where(lane >= offset, value, 0.0)
                tiles[tile + 1] += jnp.where(lane < offset, value, 0.0)
            else:
                tiles[tile] += value
    main, spare = [], [[], []]
    for tile in range(BAND // 128):
        stack = jnp.concatenate([tiles[band * 7 + tile][:6] for band in range(3)], axis=0)
        main.append(stack[:16])
        spare[0].append(stack[16:17])
        spare[1].append(stack[17:])
    spare = jnp.concatenate(spare[0] + spare[1] + [jnp.zeros((2, 128), F32)], axis=0)
    piece_ref[...] = jnp.concatenate(main + [spare], axis=1).astype(BF16)


def block_body(before_ref, own_ref, pack_ref, gain_ref, out_ref):
    early = activated(before_ref[...], gain_ref[...].reshape(1, 384))
    turned = jnp.concatenate([early, own_ref[...].astype(F32)], axis=0).T
    later = pltpu.roll(turned, 96, 1).astype(BF16)
    turned = turned.astype(BF16)
    for row in range(4):
        for core in range(2):
            whole = later if core else turned
            for width in range(4):
                out_ref[width, row, core, :SLOT, :] = whole[width * SLOT : width * SLOT + SLOT]
                out_ref[width, row, core, SLOT:, :] = pack_ref[row, core]


def grid_place(row):
    frame = row // 32 % 4
    target = frame * 128 + row // 16 % 2 * 64 + row // 128 * 16 + row % 16
    return jnp.where(frame < 3, target, -1)


def main_place(row):
    part = row // SLOT * 6 + row % 6
    return jnp.where(part < 16, row % SLOT // 6 * 16 + part, -1)


def spare_place(tile, row):
    part = row % 6 - 4
    return jnp.where(part >= 0, row // 6 * 16 + part * 7 + tile, -1)


def conv_body(place_ref, cells_ref, weight_ref, out_ref, latent_ref, flat_ref):
    lane = lax.broadcasted_iota(jnp.int32, (8 * SLOT, 128), 1) % 64
    rows = [
        jnp.concatenate([cells_ref[width, height, :SLOT, :] for height in range(8)], axis=0)
        for width in range(4)
    ]
    grid = jnp.dot(
        jnp.concatenate(rows, axis=1), one_hot((512, 384), grid_place), preferred_element_type=F32
    )
    for time_tap in range(3):
        still = grid[:, time_tap * 128 : time_tap * 128 + 128]
        left = jnp.where(lane == 0, 0.0, pltpu.roll(still, 1, 1))
        right = jnp.where(lane == 63, 0.0, pltpu.roll(still, 127, 1))
        for col_tap, base in enumerate((left, still, right)):
            slot = (time_tap * 3 + col_tap) * SLOT
            base = base.astype(BF16)
            for height in range(8):
                flat_ref[slot : slot + SLOT, height * 128 : height * 128 + 128] = base[
                    height * SLOT : height * SLOT + SLOT
                ]
    flat_ref[9 * SLOT :, :] = jnp.zeros((BAND - 9 * SLOT, 1024), BF16)
    main = jnp.dot(one_hot((3 * SLOT, 256), main_place), weight_ref[:, :BAND], preferred_element_type=F32)
    spare = [
        jnp.dot(
            one_hot((SLOT, 256), functools.partial(spare_place, tile)),
            weight_ref[:, BAND:],
            preferred_element_type=F32,
        )
        for tile in range(BAND // 128)
    ]
    last = main[2 * SLOT :] + jnp.concatenate(spare, axis=1)
    weight = jnp.concatenate([main[: 2 * SLOT], last], axis=0).astype(BF16)
    whole = jnp.dot(weight, flat_ref[...], preferred_element_type=F32)
    lane = lax.broadcasted_iota(jnp.int32, (SLOT, 1024), 1)
    total = whole[SLOT : 2 * SLOT]
    total += jnp.where(lane < 64, 0.0, pltpu.roll(whole[:SLOT], 64, 1))
    total += jnp.where(lane < 960, pltpu.roll(whole[2 * SLOT :], 960, 1), 0.0)
    pieces = [total[:, part * 256 : part * 256 + 256].T for part in range(4)]
    for width in range(4):
        rows = [
            pieces[row // 4][row % 4 * 64 + width * 16 : row % 4 * 64 + width * 16 + 16] for row in range(16)
        ]
        out_ref[width] = jnp.concatenate(rows, axis=0).T.astype(BF16)
    lane = lax.broadcasted_iota(jnp.int32, (GROUP, 128), 1)
    for member in range(4):
        for tile in range(2):
            packed = jnp.zeros((GROUP, 128), F32)
            for height in range(4):
                part = cells_ref[place_ref[3], tile * 4 + height].astype(F32)[SLOT:]
                shift = (32 * height - 32 * member) % 128
                part = pltpu.roll(part, shift, 1) if shift else part
                packed += jnp.where((lane >= 32 * height) & (lane < 32 * height + 32), part, 0.0)
            latent_ref[member * GROUP : member * GROUP + GROUP, tile * 128 : tile * 128 + 128] = packed


def hidden_body(part_ref, latent_ref, out_ref):
    summed = latent_ref[...]
    for source in range(4):
        summed += part_ref[source].astype(F32)
    hidden = summed.astype(BF16)
    for target in range(16):
        out_ref[target] = hidden


def fold_body(w_ref, w_out_ref, row_ref, column_ref, score_ref, update_ref):
    order = one_hot((384, 384), channel_of)
    gain = column_ref[...]
    score = lax.dot_general(
        w_ref[:, :384], w_ref[:, 384:768], (((1,), (1,)), ((), ())), preferred_element_type=F32
    )
    score = (score * (gain * (1.0 / 384.0**0.5)) * row_ref[...]).astype(BF16)
    score = jnp.dot(order, score, preferred_element_type=F32).astype(BF16)
    score = lax.dot_general(score, order, (((1,), (1,)), ((), ())), preferred_element_type=F32)
    score_ref[...] = score.astype(BF16)
    update = jnp.dot(w_ref[:, 768:], w_out_ref[...], preferred_element_type=F32) * gain
    update_ref[...] = jnp.dot(order, update.astype(BF16), preferred_element_type=F32).astype(BF16)


def attend_body(place_ref, block_ref, score_ref, update_ref, keep_ref, send_ref):
    own = block_ref[place_ref[3]]
    own = jnp.where(place_ref[1] < 2, own[:, :128], own[:, 128:]).astype(F32).T
    own = jnp.where(place_ref[1] % 2 == 0, own[:64], own[64:])
    own_scale = lax.rsqrt(jnp.mean(own * own, axis=-1, keepdims=True) + 1e-06)
    own = own.astype(BF16)
    query = jnp.dot(own, score_ref[...], preferred_element_type=F32)
    query = (query * own_scale).astype(BF16)
    hidden = jnp.dot(own, one_hot((384, 384), channel_of), preferred_element_type=F32)
    scales, scores = [], []
    for width in range(4):
        cells = block_ref[width]
        values = cells.astype(F32)
        scale = lax.rsqrt(jnp.mean(values * values, axis=0, keepdims=True) + 1e-06)
        scales.append(scale)
        scores.append(jnp.dot(query, cells, preferred_element_type=F32) * scale)
    peak = functools.reduce(jnp.maximum, [jnp.max(part, axis=-1, keepdims=True) for part in scores])
    total = jnp.zeros((64, 1), F32)
    mixed = jnp.zeros((64, 384), F32)
    for width in range(4):
        powers = jnp.exp(scores[width] - peak)
        total += jnp.sum(powers, axis=-1, keepdims=True)
        powers = (powers * scales[width]).astype(BF16)
        mixed += lax.dot_general(
            powers, block_ref[width], (((1,), (1,)), ((), ())), preferred_element_type=F32
        )
    mixed = (mixed / total).astype(BF16)
    decoded = (hidden + jnp.dot(mixed, update_ref[...], preferred_element_type=F32)).astype(BF16)
    first = place_ref[2] == 0
    keep_ref[...] = jnp.where(first, decoded[:32], decoded[32:])
    send_ref[...] = jnp.where(first, decoded[32:], decoded[:32])


def rms_scale(values, gain):
    mean_sq = jnp.mean(values * values, axis=-1, keepdims=True)
    return values * lax.rsqrt(mean_sq + 1e-06) * gain


def local(latent, norm_gain, conv_weight, attn_gain, w_qkv, w_out):
    channels = 384
    core = lax.axis_index("core")
    place = [lax.axis_index("tm"), lax.axis_index("y"), core, lax.axis_index("width")]
    place = jnp.stack(place).astype(jnp.int32)
    swap = [(0, 1), (1, 0)]
    shape = jax.ShapeDtypeStruct
    with jax.named_scope("earlier_frames"):
        cells = latent.reshape(64, channels)
        before = lax.ppermute(cells, "tm", [(i, i + 1) for i in range(15)])
    with jax.named_scope("activated"):
        turned = jnp.transpose(conv_weight.reshape(TAPS, channels, GROUP), (0, 2, 1))
        piece, now, pack = call(
            first_body,
            [shape((16, 1024), BF16), shape((64, channels), BF16), shape((4, 2, GROUP, 128), BF16)],
            [SMEM, HBM, HBM, HBM],
            scratch=[
                pltpu.VMEM((TAPS, GROUP, channels), BF16),
                pltpu.VMEM((64, channels), BF16),
                pltpu.VMEM((channels,), F32),
                pltpu.SemaphoreType.DMA((3,)),
            ],
            limit=FIRST_LIMIT,
        )(place, turned, cells, norm_gain)
        blocks = call(block_body, shape((4, 4, 2, SLOT + GROUP, 128), BF16), [VMEM] * 4)(
            before, now, pack, norm_gain
        )
        piece, blocks = lax.optimization_barrier((piece, blocks))
        weight = lax.all_gather(piece, "tm", axis=0, tiled=True)
        blocks = lax.all_to_all(blocks.reshape(32, SLOT + GROUP, 128), ("width", "y", "core"), 0, 0)
    with jax.named_scope("conv"):
        parts, own = call(
            conv_body,
            [shape((4, SLOT, 256), BF16), shape((SLOT, 256), F32)],
            [SMEM, VMEM, VMEM],
            700_000_000,
            scratch=[pltpu.VMEM((BAND, 1024), BF16)],
        )(place, blocks.reshape(4, 8, SLOT + GROUP, 128), weight)
        parts = lax.all_to_all(parts, "width", 0, 0)
    with jax.named_scope("hidden"):
        hidden = call(hidden_body, shape((16, SLOT, 256), BF16), [VMEM] * 2)(parts, own)
        hidden = lax.all_to_all(hidden, PLANE, 0, 0)
    with jax.named_scope("attention"):
        square, half = shape((channels, channels), BF16), shape((32, channels), BF16)
        score, update = call(fold_body, [square, square], [VMEM] * 4, 600_000_000)(
            w_qkv, w_out, attn_gain.reshape(1, channels), attn_gain.reshape(channels, 1)
        )
        keep, send = call(attend_body, [half, half], [SMEM] + [VMEM] * 3, 200_000_000)(
            place, hidden.reshape(4, channels, 256), score, update
        )
        got = lax.ppermute(send, "core", swap)
        out = jnp.where(core == 0, jnp.concatenate([keep, got]), jnp.concatenate([got, keep]))
    return out.reshape(latent.shape)


def solution(mesh):
    devices = mesh.devices.reshape(16, 4, 2, 4)
    fine = Mesh(devices, ("tm", "y", "core", "width"))
    cells = P("tm", ("y", "core"), "width", None)
    in_specs = (cells, P(), P(None, None, None, None, "tm"), P(), P(), P())
    return jax.shard_map(local, mesh=fine, in_specs=in_specs, out_specs=cells, check_vma=False)
```

```python
import functools

import jax
import jax.numpy as jnp
from jax import lax
from jax.experimental import pallas as pl
from jax.experimental.pallas import tpu as pltpu
from jax.sharding import Mesh, PartitionSpec as P

F32 = jnp.float32
BF16 = jnp.bfloat16
TAPS = 27
GROUP = 24
SLOT = 96
BAND = 896
PLANE = ("width", "y")
VMEM = pl.BlockSpec(memory_space=pltpu.VMEM)
SMEM = pl.BlockSpec(memory_space=pltpu.SMEM)
LIMIT = 12 * 1024 * 1024


def call(body, out, specs, flops=1_000_000, moved=1_000_000, scratch=()):
    many = isinstance(out, (tuple, list))
    return pl.pallas_call(
        body,
        out_shape=out,
        in_specs=specs,
        out_specs=[VMEM] * len(out) if many else VMEM,
        scratch_shapes=list(scratch),
        compiler_params=pltpu.CompilerParams(vmem_limit_bytes=LIMIT),
        cost_estimate=pl.CostEstimate(flops=flops, bytes_accessed=moved, transcendentals=0),
    )


def one_hot(shape, column_of):
    row = lax.broadcasted_iota(jnp.int32, (shape[0], 1), 0)
    col = lax.broadcasted_iota(jnp.int32, shape, 1)
    return (col == column_of(row)).astype(F32).astype(BF16)


def channel_of(place):
    return place % SLOT // 6 * GROUP + place // SLOT * 6 + place % 6


def activated(values, gain):
    scaled = rms_scale(values.astype(F32), gain)
    return scaled / (1.0 + jnp.exp(-scaled))


def weight_body(place_ref, weight_ref, piece_ref):
    start = place_ref[3] * SLOT
    pick = one_hot((384, 128), lambda row: jnp.where(row - start < SLOT, row - start, -1))
    rows = jnp.concatenate([weight_ref[tap] for tap in range(TAPS)], axis=0)
    picked = jnp.dot(rows, pick, preferred_element_type=F32)
    upper = place_ref[1] // 2
    picked = jnp.where(upper == 0, picked, pltpu.roll(picked, TAPS * GROUP - 12, 0))
    picked = jnp.where(place_ref[1] % 2 == 0, picked, pltpu.roll(picked, TAPS * GROUP - 6, 0))
    lane = lax.broadcasted_iota(jnp.int32, (8, 128), 1)
    kept = lax.broadcasted_iota(jnp.int32, (8, 128), 0) < 6
    tiles = [jnp.zeros((8, 128), F32) for _ in range(3 * BAND // 128)]
    for row_tap in range(3):
        for slot in range(9):
            tap = slot // 3 * 9 + row_tap * 3 + slot % 3
            value = jnp.where(kept, picked[tap * GROUP : tap * GROUP + 8], 0.0)
            tile, offset = divmod(row_tap * BAND + slot * SLOT, 128)
            value = pltpu.roll(value, offset, 1) if offset else value
            if offset + SLOT > 128:
                tiles[tile] += jnp.where(lane >= offset, value, 0.0)
                tiles[tile + 1] += jnp.where(lane < offset, value, 0.0)
            else:
                tiles[tile] += value
    main, spare = [], [[], []]
    for tile in range(BAND // 128):
        stack = jnp.concatenate([tiles[band * 7 + tile][:6] for band in range(3)], axis=0)
        main.append(stack[:16])
        spare[0].append(stack[16:17])
        spare[1].append(stack[17:])
    spare = jnp.concatenate(spare[0] + spare[1] + [jnp.zeros((2, 128), F32)], axis=0)
    piece_ref[...] = jnp.concatenate(main + [spare], axis=1).astype(BF16)


def activated(values, gain):
    scaled = rms_scale(values.astype(F32), gain)
    return scaled / (1.0 + jnp.exp(-scaled))


def by_frame(ref):
    return jnp.concatenate([ref[0:32], ref[64:96], ref[32:64], ref[96:128]], axis=0)


def block_body(before_ref, now_ref, gain_ref, out_ref):
    now = by_frame(now_ref)
    both = activated(jnp.concatenate([by_frame(before_ref), now], axis=0), gain_ref[...]).T.astype(BF16)
    latent = lax.dot_general(
        one_hot((384, 384), channel_of), now, (((1,), (1,)), ((), ())), preferred_element_type=F32
    )
    blank = jnp.zeros((GROUP, 128), BF16)
    for width in range(4):
        for row in range(4):
            start = row * SLOT + width * GROUP
            out_ref[width, row, :SLOT, :] = both[width * SLOT : width * SLOT + SLOT]
            out_ref[width, row, SLOT:, :128] = latent[start : start + GROUP].astype(BF16)
            out_ref[width, row, SLOT:, 128:] = blank


def grid_place(odd, row):
    target = row // 16 % 4 * 64 + row // 128 * 16 + row % 16
    return jnp.where(row // 64 % 2 == odd, target, -1)


def patch_body(place_ref, mine_ref, handed_ref, flat_ref, latent_ref):
    core = place_ref[2]
    lane = lax.broadcasted_iota(jnp.int32, (4 * SLOT, 256), 1) % 64
    blocks = [[None] * 4 for _ in range(4)]
    for width in range(4):
        for row in range(4):
            blocks[row][width] = jnp.where(core == 0, mine_ref[width, row], handed_ref[width, row])
    places = [one_hot((512, 256), functools.partial(grid_place, odd)) for odd in range(2)]
    frames = []
    for pair in range(2):
        cut = slice(pair * 128, pair * 128 + 128)
        rows = [
            jnp.concatenate([blocks[row][width][:SLOT, cut] for width in range(4)], axis=1) for row in range(4)
        ]
        rows = jnp.concatenate(rows, axis=0)
        frames += [jnp.dot(rows, place, preferred_element_type=F32) for place in places]
    for time_tap in range(3):
        still = jnp.where(core == 0, frames[time_tap], frames[time_tap + 1])
        left = jnp.where(lane == 0, 0.0, pltpu.roll(still, 1, 1))
        right = jnp.where(lane == 63, 0.0, pltpu.roll(still, 255, 1))
        for col_tap, base in enumerate((left, still, right)):
            slot = (time_tap * 3 + col_tap) * SLOT
            base = base.astype(BF16)
            for row in range(4):
                flat_ref[slot : slot + SLOT, row * 256 : row * 256 + 256] = base[row * SLOT : row * SLOT + SLOT]
    flat_ref[9 * SLOT :, :] = jnp.zeros((BAND - 9 * SLOT, 1024), BF16)
    place = jnp.where(core == 0, places[0], places[1])
    for row in range(4):
        part = jnp.concatenate([blocks[row][width][SLOT:, :128] for width in range(4)], axis=1)
        latent_ref[:, row * 256 : row * 256 + 256] = jnp.dot(part, place, preferred_element_type=F32)


def main_place(row):
    part = row // SLOT * 6 + row % 6
    return jnp.where(part < 16, row % SLOT // 6 * 16 + part, -1)


def spare_place(tile, row):
    part = row % 6 - 4
    return jnp.where(part >= 0, row // 6 * 16 + part * 7 + tile, -1)


def conv_body(place_ref, flat_ref, latent_ref, mine_ref, handed_ref, out_ref):
    gathered = jnp.where(place_ref[2] == 1, mine_ref[...], handed_ref[...])
    main = jnp.dot(one_hot((3 * SLOT, 256), main_place), gathered[:, :BAND], preferred_element_type=F32)
    spare = [
        jnp.dot(
            one_hot((SLOT, 256), functools.partial(spare_place, tile)),
            gathered[:, BAND:],
            preferred_element_type=F32,
        )
        for tile in range(BAND // 128)
    ]
    last = main[2 * SLOT :] + jnp.concatenate(spare, axis=1)
    weight = jnp.concatenate([main[: 2 * SLOT], last], axis=0).astype(BF16)
    whole = jnp.dot(weight, flat_ref[...], preferred_element_type=F32)
    lane = lax.broadcasted_iota(jnp.int32, (SLOT, 1024), 1)
    total = whole[SLOT : 2 * SLOT]
    total += jnp.where(lane < 64, 0.0, pltpu.roll(whole[:SLOT], 64, 1))
    total += jnp.where(lane < 960, pltpu.roll(whole[2 * SLOT :], 960, 1), 0.0)
    owner = lax.broadcasted_iota(jnp.int32, (SLOT, 1024), 0) // GROUP
    total += jnp.where(owner == place_ref[3], jnp.concatenate([latent_ref[...]] * 4, axis=0), 0.0)
    pieces = [total[:, part * 256 : part * 256 + 256].T for part in range(4)]
    for width in range(4):
        rows = [
            pieces[row // 4][row % 4 * 64 + width * 16 : row % 4 * 64 + width * 16 + 16] for row in range(16)
        ]
        out_ref[width] = jnp.concatenate(rows, axis=0).T.astype(BF16)


def hidden_body(part_ref, out_ref):
    summed = part_ref[0].astype(F32)
    for source in range(1, 4):
        summed += part_ref[source].astype(F32)
    hidden = summed.astype(BF16)
    for target in range(16):
        out_ref[target] = hidden


def fold_body(w_ref, w_out_ref, row_ref, column_ref, score_ref, update_ref):
    order = one_hot((384, 384), channel_of)
    gain = column_ref[...]
    score = lax.dot_general(
        w_ref[:, :384], w_ref[:, 384:768], (((1,), (1,)), ((), ())), preferred_element_type=F32
    )
    score = (score * (gain * (1.0 / 384.0**0.5)) * row_ref[...]).astype(BF16)
    score = jnp.dot(order, score, preferred_element_type=F32).astype(BF16)
    score = lax.dot_general(score, order, (((1,), (1,)), ((), ())), preferred_element_type=F32)
    score_ref[...] = score.astype(BF16)
    update = jnp.dot(w_ref[:, 768:], w_out_ref[...], preferred_element_type=F32) * gain
    update_ref[...] = jnp.dot(order, update.astype(BF16), preferred_element_type=F32).astype(BF16)


def attend_body(place_ref, block_ref, score_ref, update_ref, keep_ref, send_ref):
    own = block_ref[place_ref[3]]
    own = jnp.where(place_ref[1] < 2, own[:, :128], own[:, 128:]).astype(F32).T
    own = jnp.where(place_ref[1] % 2 == 0, own[:64], own[64:])
    own_scale = lax.rsqrt(jnp.mean(own * own, axis=-1, keepdims=True) + 1e-06)
    own = own.astype(BF16)
    query = jnp.dot(own, score_ref[...], preferred_element_type=F32)
    query = (query * own_scale).astype(BF16)
    hidden = jnp.dot(own, one_hot((384, 384), channel_of), preferred_element_type=F32)
    scales, scores = [], []
    for width in range(4):
        cells = block_ref[width]
        values = cells.astype(F32)
        scale = lax.rsqrt(jnp.mean(values * values, axis=0, keepdims=True) + 1e-06)
        scales.append(scale)
        scores.append(jnp.dot(query, cells, preferred_element_type=F32) * scale)
    peak = functools.reduce(jnp.maximum, [jnp.max(part, axis=-1, keepdims=True) for part in scores])
    total = jnp.zeros((64, 1), F32)
    mixed = jnp.zeros((64, 384), F32)
    for width in range(4):
        powers = jnp.exp(scores[width] - peak)
        total += jnp.sum(powers, axis=-1, keepdims=True)
        powers = (powers * scales[width]).astype(BF16)
        mixed += lax.dot_general(
            powers, block_ref[width], (((1,), (1,)), ((), ())), preferred_element_type=F32
        )
    mixed = (mixed / total).astype(BF16)
    decoded = (hidden + jnp.dot(mixed, update_ref[...], preferred_element_type=F32)).astype(BF16)
    first = place_ref[2] == 0
    keep_ref[...] = jnp.where(first, decoded[:32], decoded[32:])
    send_ref[...] = jnp.where(first, decoded[32:], decoded[:32])


def rms_scale(values, gain):
    mean_sq = jnp.mean(values * values, axis=-1, keepdims=True)
    return values * lax.rsqrt(mean_sq + 1e-06) * gain


def local(latent, norm_gain, conv_weight, attn_gain, w_qkv, w_out):
    channels = 384
    core = lax.axis_index("core")
    place = [lax.axis_index("tm"), lax.axis_index("y"), core, lax.axis_index("width")]
    place = jnp.stack(place).astype(jnp.int32)
    swap = [(0, 1), (1, 0)]
    shape = jax.ShapeDtypeStruct
    cells = latent.reshape(64, channels)
    weight_shape, block_shape = (256, 1024), (16, SLOT + GROUP, 256)

    def gather_weights(cells, lower, gain, turned):
        piece = call(weight_body, shape((16, 1024), BF16), [SMEM, VMEM])(place, turned)
        weight = lax.all_gather(piece, "tm", axis=0, tiled=True)
        return weight, jnp.zeros(block_shape, BF16)

    def exchange_cells(cells, lower, gain, turned):
        now = jnp.concatenate([cells, lower], axis=0)
        before = lax.ppermute(now, ("tm", "core"), [(2 * i, 2 * i + 2) for i in range(15)])
        blocks = call(block_body, shape((4, 4, SLOT + GROUP, 256), BF16), [VMEM] * 3)(before, now, gain)
        return jnp.zeros(weight_shape, BF16), lax.all_to_all(blocks.reshape(block_shape), PLANE, 0, 0)

    with jax.named_scope("weights_and_cells"):
        lower = lax.ppermute(cells, "core", [(1, 0)])
        turned = jnp.transpose(conv_weight.reshape(TAPS, channels, GROUP), (0, 2, 1))
        weight, blocks = lax.cond(
            core == 1, gather_weights, exchange_cells, cells, lower, norm_gain.reshape(1, channels), turned
        )
    with jax.named_scope("patches"):
        handed_blocks = lax.ppermute(blocks, "core", [(0, 1)])
        handed_weight = lax.ppermute(weight, "core", [(1, 0)])
        grouped = (4, 4, SLOT + GROUP, 256)
        flat, own = call(
            patch_body, [shape((BAND, 1024), BF16), shape((GROUP, 1024), F32)], [SMEM] + [VMEM] * 2
        )(place, blocks.reshape(grouped), handed_blocks.reshape(grouped))
    with jax.named_scope("conv"):
        parts = call(conv_body, shape((4, SLOT, 256), BF16), [SMEM] + [VMEM] * 4, 700_000_000)(
            place, flat, own, weight, handed_weight
        )
        parts = lax.all_to_all(parts, "width", 0, 0)
    with jax.named_scope("hidden"):
        hidden = call(hidden_body, shape((16, SLOT, 256), BF16), [VMEM])(parts)
        hidden = lax.all_to_all(hidden, PLANE, 0, 0)
    with jax.named_scope("attention"):
        square, half = shape((channels, channels), BF16), shape((32, channels), BF16)
        score, update = call(fold_body, [square, square], [VMEM] * 4, 600_000_000)(
            w_qkv, w_out, attn_gain.reshape(1, channels), attn_gain.reshape(channels, 1)
        )
        keep, send = call(attend_body, [half, half], [SMEM] + [VMEM] * 3, 200_000_000)(
            place, hidden.reshape(4, channels, 256), score, update
        )
        got = lax.ppermute(send, "core", swap)
        out = jnp.where(core == 0, jnp.concatenate([keep, got]), jnp.concatenate([got, keep]))
    return out.reshape(latent.shape)


def solution(mesh):
    devices = mesh.devices.reshape(16, 4, 2, 4)
    fine = Mesh(devices, ("tm", "y", "core", "width"))
    cells = P("tm", ("y", "core"), "width", None)
    in_specs = (cells, P(), P(None, None, None, None, "tm"), P(), P(), P())
    return jax.shard_map(local, mesh=fine, in_specs=in_specs, out_specs=cells, check_vma=False)
```

```python
import functools

import jax
import jax.numpy as jnp
from jax import lax
from jax.experimental import pallas as pl
from jax.experimental.pallas import tpu as pltpu
from jax.sharding import Mesh, PartitionSpec as P

F32 = jnp.float32
BF16 = jnp.bfloat16
TAPS = 27
GROUP = 24
SLOT = 96
BAND = 896
PLANE = ("width", "y")
VMEM = pl.BlockSpec(memory_space=pltpu.VMEM)
SMEM = pl.BlockSpec(memory_space=pltpu.SMEM)
LIMIT = 12 * 1024 * 1024


def call(body, out, specs, flops=1_000_000, moved=1_000_000, scratch=()):
    many = isinstance(out, (tuple, list))
    return pl.pallas_call(
        body,
        out_shape=out,
        in_specs=specs,
        out_specs=[VMEM] * len(out) if many else VMEM,
        scratch_shapes=list(scratch),
        compiler_params=pltpu.CompilerParams(vmem_limit_bytes=LIMIT),
        cost_estimate=pl.CostEstimate(flops=flops, bytes_accessed=moved, transcendentals=0),
    )


def one_hot(shape, column_of):
    row = lax.broadcasted_iota(jnp.int32, (shape[0], 1), 0)
    col = lax.broadcasted_iota(jnp.int32, shape, 1)
    return (col == column_of(row)).astype(F32).astype(BF16)


def channel_of(place):
    return place % SLOT // 6 * GROUP + place // SLOT * 6 + place % 6


def activated(values, gain):
    scaled = rms_scale(values.astype(F32), gain)
    return scaled / (1.0 + jnp.exp(-scaled))


def weight_body(place_ref, weight_ref, piece_ref):
    start = place_ref[3] * SLOT
    pick = one_hot((384, 128), lambda row: jnp.where(row - start < SLOT, row - start, -1))
    rows = jnp.concatenate([weight_ref[tap] for tap in range(TAPS)], axis=0)
    picked = jnp.dot(rows, pick, preferred_element_type=F32)
    upper = place_ref[1] // 2
    picked = jnp.where(upper == 0, picked, pltpu.roll(picked, TAPS * GROUP - 12, 0))
    picked = jnp.where(place_ref[1] % 2 == 0, picked, pltpu.roll(picked, TAPS * GROUP - 6, 0))
    lane = lax.broadcasted_iota(jnp.int32, (8, 128), 1)
    kept = lax.broadcasted_iota(jnp.int32, (8, 128), 0) < 6
    tiles = [jnp.zeros((8, 128), F32) for _ in range(3 * BAND // 128)]
    for row_tap in range(3):
        for slot in range(9):
            tap = slot // 3 * 9 + row_tap * 3 + slot % 3
            value = jnp.where(kept, picked[tap * GROUP : tap * GROUP + 8], 0.0)
            tile, offset = divmod(row_tap * BAND + slot * SLOT, 128)
            value = pltpu.roll(value, offset, 1) if offset else value
            if offset + SLOT > 128:
                tiles[tile] += jnp.where(lane >= offset, value, 0.0)
                tiles[tile + 1] += jnp.where(lane < offset, value, 0.0)
            else:
                tiles[tile] += value
    main, spare = [], [[], []]
    for tile in range(BAND // 128):
        stack = jnp.concatenate([tiles[band * 7 + tile][:6] for band in range(3)], axis=0)
        main.append(stack[:16])
        spare[0].append(stack[16:17])
        spare[1].append(stack[17:])
    spare = jnp.concatenate(spare[0] + spare[1] + [jnp.zeros((2, 128), F32)], axis=0)
    piece_ref[...] = jnp.concatenate(main + [spare], axis=1).astype(BF16)


def activated(values, gain):
    scaled = rms_scale(values.astype(F32), gain)
    return scaled / (1.0 + jnp.exp(-scaled))


def by_frame(ref):
    return jnp.concatenate([ref[0:32], ref[64:96], ref[32:64], ref[96:128]], axis=0)


def block_body(before_ref, now_ref, gain_ref, out_ref):
    now = by_frame(now_ref)
    both = activated(jnp.concatenate([by_frame(before_ref), now], axis=0), gain_ref[...]).T.astype(BF16)
    latent = lax.dot_general(
        one_hot((384, 384), channel_of), now, (((1,), (1,)), ((), ())), preferred_element_type=F32
    )
    blank = jnp.zeros((GROUP, 128), BF16)
    for width in range(4):
        for row in range(4):
            start = row * SLOT + width * GROUP
            out_ref[width, row, :SLOT, :] = both[width * SLOT : width * SLOT + SLOT]
            out_ref[width, row, SLOT:, :128] = latent[start : start + GROUP].astype(BF16)
            out_ref[width, row, SLOT:, 128:] = blank


def grid_place(odd, row):
    target = row // 16 % 4 * 64 + row // 128 * 16 + row % 16
    return jnp.where(row // 64 % 2 == odd, target, -1)


def patch_body(place_ref, mine_ref, handed_ref, flat_ref, latent_ref):
    core = place_ref[2]
    lane = lax.broadcasted_iota(jnp.int32, (4 * SLOT, 256), 1) % 64
    blocks = [[None] * 4 for _ in range(4)]
    for width in range(4):
        for row in range(4):
            blocks[row][width] = jnp.where(core == 0, mine_ref[width, row], handed_ref[width, row])
    places = [one_hot((512, 256), functools.partial(grid_place, odd)) for odd in range(2)]
    frames = []
    for pair in range(2):
        cut = slice(pair * 128, pair * 128 + 128)
        rows = [
            jnp.concatenate([blocks[row][width][:SLOT, cut] for width in range(4)], axis=1) for row in range(4)
        ]
        rows = jnp.concatenate(rows, axis=0)
        frames += [jnp.dot(rows, place, preferred_element_type=F32) for place in places]
    for time_tap in range(3):
        still = jnp.where(core == 0, frames[time_tap], frames[time_tap + 1])
        left = jnp.where(lane == 0, 0.0, pltpu.roll(still, 1, 1))
        right = jnp.where(lane == 63, 0.0, pltpu.roll(still, 255, 1))
        for col_tap, base in enumerate((left, still, right)):
            slot = (time_tap * 3 + col_tap) * SLOT
            base = base.astype(BF16)
            for row in range(4):
                flat_ref[slot : slot + SLOT, row * 256 : row * 256 + 256] = base[row * SLOT : row * SLOT + SLOT]
    flat_ref[9 * SLOT :, :] = jnp.zeros((BAND - 9 * SLOT, 1024), BF16)
    place = jnp.where(core == 0, places[0], places[1])
    for row in range(4):
        part = jnp.concatenate([blocks[row][width][SLOT:, :128] for width in range(4)], axis=1)
        latent_ref[:, row * 256 : row * 256 + 256] = jnp.dot(part, place, preferred_element_type=F32)


def main_place(row):
    part = row // SLOT * 6 + row % 6
    return jnp.where(part < 16, row % SLOT // 6 * 16 + part, -1)


def spare_place(tile, row):
    part = row % 6 - 4
    return jnp.where(part >= 0, row // 6 * 16 + part * 7 + tile, -1)


def conv_body(place_ref, flat_ref, latent_ref, mine_ref, handed_ref, out_ref):
    gathered = jnp.where(place_ref[2] == 1, mine_ref[...], handed_ref[...])
    main = jnp.dot(one_hot((3 * SLOT, 256), main_place), gathered[:, :BAND], preferred_element_type=F32)
    spare = [
        jnp.dot(
            one_hot((SLOT, 256), functools.partial(spare_place, tile)),
            gathered[:, BAND:],
            preferred_element_type=F32,
        )
        for tile in range(BAND // 128)
    ]
    last = main[2 * SLOT :] + jnp.concatenate(spare, axis=1)
    weight = jnp.concatenate([main[: 2 * SLOT], last], axis=0).astype(BF16)
    whole = jnp.dot(weight, flat_ref[...], preferred_element_type=F32)
    lane = lax.broadcasted_iota(jnp.int32, (SLOT, 1024), 1)
    total = whole[SLOT : 2 * SLOT]
    total += jnp.where(lane < 64, 0.0, pltpu.roll(whole[:SLOT], 64, 1))
    total += jnp.where(lane < 960, pltpu.roll(whole[2 * SLOT :], 960, 1), 0.0)
    owner = lax.broadcasted_iota(jnp.int32, (SLOT, 1024), 0) // GROUP
    total += jnp.where(owner == place_ref[3], jnp.concatenate([latent_ref[...]] * 4, axis=0), 0.0)
    pieces = [total[:, part * 256 : part * 256 + 256].T for part in range(4)]
    for width in range(4):
        rows = [
            pieces[row // 4][row % 4 * 64 + width * 16 : row % 4 * 64 + width * 16 + 16] for row in range(16)
        ]
        out_ref[width] = jnp.concatenate(rows, axis=0).T.astype(BF16)


def hidden_body(part_ref, out_ref):
    summed = part_ref[0].astype(F32)
    for source in range(1, 4):
        summed += part_ref[source].astype(F32)
    hidden = summed.astype(BF16)
    for target in range(16):
        out_ref[target] = hidden


def fold_body(w_ref, w_out_ref, row_ref, column_ref, score_ref, update_ref, order_ref):
    order = one_hot((384, 384), channel_of)
    order_ref[...] = order
    gain = column_ref[...]
    score = lax.dot_general(
        w_ref[:, :384], w_ref[:, 384:768], (((1,), (1,)), ((), ())), preferred_element_type=F32
    )
    score = (score * (gain * (1.0 / 384.0**0.5)) * row_ref[...]).astype(BF16)
    score = jnp.dot(order, score, preferred_element_type=F32).astype(BF16)
    score = lax.dot_general(score, order, (((1,), (1,)), ((), ())), preferred_element_type=F32)
    score_ref[...] = score.astype(BF16)
    update = jnp.dot(w_ref[:, 768:], w_out_ref[...], preferred_element_type=F32) * gain
    update_ref[...] = jnp.dot(order, update.astype(BF16), preferred_element_type=F32).astype(BF16)


def attend_body(place_ref, block_ref, score_ref, update_ref, order_ref, keep_ref, send_ref):
    own = block_ref[place_ref[3]]
    own = jnp.where(place_ref[1] < 2, own[:, :128], own[:, 128:]).astype(F32).T
    own = jnp.where(place_ref[1] % 2 == 0, own[:64], own[64:])
    own_scale = lax.rsqrt(jnp.mean(own * own, axis=-1, keepdims=True) + 1e-06)
    own = own.astype(BF16)
    query = jnp.dot(own, score_ref[...], preferred_element_type=F32)
    query = (query * own_scale).astype(BF16)
    hidden = jnp.dot(own, order_ref[...], preferred_element_type=F32)
    scales, scores = [], []
    for width in range(4):
        cells = block_ref[width]
        values = cells.astype(F32)
        scale = lax.rsqrt(jnp.mean(values * values, axis=0, keepdims=True) + 1e-06)
        scales.append(scale)
        scores.append(jnp.dot(query, cells, preferred_element_type=F32) * scale)
    peak = functools.reduce(jnp.maximum, [jnp.max(part, axis=-1, keepdims=True) for part in scores])
    total = jnp.zeros((64, 1), F32)
    mixed = jnp.zeros((64, 384), F32)
    for width in range(4):
        powers = jnp.exp(scores[width] - peak)
        total += jnp.sum(powers, axis=-1, keepdims=True)
        powers = (powers * scales[width]).astype(BF16)
        mixed += lax.dot_general(
            powers, block_ref[width], (((1,), (1,)), ((), ())), preferred_element_type=F32
        )
    mixed = (mixed / total).astype(BF16)
    decoded = (hidden + jnp.dot(mixed, update_ref[...], preferred_element_type=F32)).astype(BF16)
    first = place_ref[2] == 0
    keep_ref[...] = jnp.where(first, decoded[:32], decoded[32:])
    send_ref[...] = jnp.where(first, decoded[32:], decoded[:32])


def rms_scale(values, gain):
    mean_sq = jnp.mean(values * values, axis=-1, keepdims=True)
    return values * lax.rsqrt(mean_sq + 1e-06) * gain


def local(latent, norm_gain, conv_weight, attn_gain, w_qkv, w_out):
    channels = 384
    core = lax.axis_index("core")
    place = [lax.axis_index("tm"), lax.axis_index("y"), core, lax.axis_index("width")]
    place = jnp.stack(place).astype(jnp.int32)
    swap = [(0, 1), (1, 0)]
    shape = jax.ShapeDtypeStruct
    cells = latent.reshape(64, channels)
    weight_shape, block_shape = (256, 1024), (16, SLOT + GROUP, 256)

    def gather_weights(cells, lower, gain, piece):
        weight = lax.all_gather(piece, "tm", axis=0, tiled=True)
        return weight, jnp.zeros(block_shape, BF16)

    def exchange_cells(cells, lower, gain, piece):
        now = jnp.concatenate([cells, lower], axis=0)
        before = lax.ppermute(now, ("tm", "core"), [(2 * i, 2 * i + 2) for i in range(15)])
        blocks = call(block_body, shape((4, 4, SLOT + GROUP, 256), BF16), [VMEM] * 3)(before, now, gain)
        return jnp.zeros(weight_shape, BF16), lax.all_to_all(blocks.reshape(block_shape), PLANE, 0, 0)

    with jax.named_scope("weights_and_cells"):
        lower = lax.ppermute(cells, "core", [(1, 0)])
        turned = jnp.transpose(conv_weight.reshape(TAPS, channels, GROUP), (0, 2, 1))
        piece = call(weight_body, shape((16, 1024), BF16), [SMEM, VMEM])(place, turned)
        weight, blocks = lax.cond(
            core == 1, gather_weights, exchange_cells, cells, lower, norm_gain.reshape(1, channels), piece
        )
    with jax.named_scope("patches"):
        handed_blocks = lax.ppermute(blocks, "core", [(0, 1)])
        handed_weight = lax.ppermute(weight, "core", [(1, 0)])
        grouped = (4, 4, SLOT + GROUP, 256)
        flat, own = call(
            patch_body, [shape((BAND, 1024), BF16), shape((GROUP, 1024), F32)], [SMEM] + [VMEM] * 2
        )(place, blocks.reshape(grouped), handed_blocks.reshape(grouped))
    with jax.named_scope("conv"):
        parts = call(conv_body, shape((4, SLOT, 256), BF16), [SMEM] + [VMEM] * 4, 700_000_000)(
            place, flat, own, weight, handed_weight
        )
        parts = lax.all_to_all(parts, "width", 0, 0)
    with jax.named_scope("hidden"):
        hidden = call(hidden_body, shape((16, SLOT, 256), BF16), [VMEM])(parts)
        hidden = lax.all_to_all(hidden, PLANE, 0, 0)
    with jax.named_scope("attention"):
        square, half = shape((channels, channels), BF16), shape((32, channels), BF16)
        score, update, order = call(fold_body, [square] * 3, [VMEM] * 4, 600_000_000)(
            w_qkv, w_out, attn_gain.reshape(1, channels), attn_gain.reshape(channels, 1)
        )
        keep, send = call(attend_body, [half, half], [SMEM] + [VMEM] * 4, 200_000_000)(
            place, hidden.reshape(4, channels, 256), score, update, order
        )
        got = lax.ppermute(send, "core", swap)
        out = jnp.where(core == 0, jnp.concatenate([keep, got]), jnp.concatenate([got, keep]))
    return out.reshape(latent.shape)


def solution(mesh):
    devices = mesh.devices.reshape(16, 4, 2, 4)
    fine = Mesh(devices, ("tm", "y", "core", "width"))
    cells = P("tm", ("y", "core"), "width", None)
    in_specs = (cells, P(), P(None, None, None, None, "tm"), P(), P(), P())
    return jax.shard_map(local, mesh=fine, in_specs=in_specs, out_specs=cells, check_vma=False)
```

```python
import functools

import jax
import jax.numpy as jnp
from jax import lax
from jax.experimental import pallas as pl
from jax.experimental.pallas import tpu as pltpu
from jax.sharding import Mesh, PartitionSpec as P

F32 = jnp.float32
BF16 = jnp.bfloat16
TAPS = 27
GROUP = 24
SLOT = 96
ROWS = SLOT + 16
BAND = 896
PLANE = ("width", "y")
VMEM = pl.BlockSpec(memory_space=pltpu.VMEM)
SMEM = pl.BlockSpec(memory_space=pltpu.SMEM)
LIMIT = 12 * 1024 * 1024
FIRST_LIMIT = 55040 * 1024


def call(body, out, specs, flops=1_000_000, moved=1_000_000, scratch=(), limit=LIMIT):
    many = isinstance(out, (tuple, list))
    return pl.pallas_call(
        body,
        out_shape=out,
        in_specs=specs,
        out_specs=[VMEM] * len(out) if many else VMEM,
        scratch_shapes=list(scratch),
        compiler_params=pltpu.CompilerParams(vmem_limit_bytes=limit),
        cost_estimate=pl.CostEstimate(flops=flops, bytes_accessed=moved, transcendentals=0),
    )


def one_hot(shape, column_of):
    row = lax.broadcasted_iota(jnp.int32, (shape[0], 1), 0)
    col = lax.broadcasted_iota(jnp.int32, shape, 1)
    return (col == column_of(row)).astype(F32).astype(BF16)


def channel_of(place):
    return place % SLOT // 6 * GROUP + place // SLOT * 6 + place % 6


def activated(values, gain):
    scaled = rms_scale(values.astype(F32), gain)
    return scaled / (1.0 + jnp.exp(-scaled))


def weight_body(place_ref, weight_ref, piece_ref):
    start = place_ref[3] * SLOT
    pick = one_hot((384, 128), lambda row: jnp.where(row - start < SLOT, row - start, -1))
    rows = jnp.concatenate([weight_ref[tap] for tap in range(TAPS)], axis=0)
    picked = jnp.dot(rows, pick, preferred_element_type=F32)
    upper = place_ref[1] // 2
    picked = jnp.where(upper == 0, picked, pltpu.roll(picked, TAPS * GROUP - 12, 0))
    picked = jnp.where(place_ref[1] % 2 == 0, picked, pltpu.roll(picked, TAPS * GROUP - 6, 0))
    lane = lax.broadcasted_iota(jnp.int32, (8, 128), 1)
    kept = lax.broadcasted_iota(jnp.int32, (8, 128), 0) < 6
    tiles = [jnp.zeros((8, 128), F32) for _ in range(3 * BAND // 128)]
    for row_tap in range(3):
        for slot in range(9):
            tap = slot // 3 * 9 + row_tap * 3 + slot % 3
            value = jnp.where(kept, picked[tap * GROUP : tap * GROUP + 8], 0.0)
            tile, offset = divmod(row_tap * BAND + slot * SLOT, 128)
            value = pltpu.roll(value, offset, 1) if offset else value
            if offset + SLOT > 128:
                tiles[tile] += jnp.where(lane >= offset, value, 0.0)
                tiles[tile + 1] += jnp.where(lane < offset, value, 0.0)
            else:
                tiles[tile] += value
    main, spare = [], [[], []]
    for tile in range(BAND // 128):
        stack = jnp.concatenate([tiles[band * 7 + tile][:6] for band in range(3)], axis=0)
        main.append(stack[:16])
        spare[0].append(stack[16:17])
        spare[1].append(stack[17:])
    spare = jnp.concatenate(spare[0] + spare[1] + [jnp.zeros((2, 128), F32)], axis=0)
    piece_ref[...] = jnp.concatenate(main + [spare], axis=1).astype(BF16)


def activated(values, gain):
    scaled = rms_scale(values.astype(F32), gain)
    return scaled / (1.0 + jnp.exp(-scaled))


def by_frame(ref):
    return jnp.concatenate([ref[0:32], ref[64:96], ref[32:64], ref[96:128]], axis=0)


def block_body(before_ref, now_ref, gain_ref, out_ref):
    now = by_frame(now_ref)
    both = activated(jnp.concatenate([by_frame(before_ref), now], axis=0), gain_ref[...]).T.astype(BF16)
    latent = lax.dot_general(
        one_hot((384, 384), channel_of), now, (((1,), (1,)), ((), ())), preferred_element_type=F32
    )
    blank = jnp.zeros((8, 128), F32)
    for width in range(4):
        for row in range(4):
            start = row * SLOT + width * GROUP
            out_ref[width, row, :SLOT, :] = both[width * SLOT : width * SLOT + SLOT]
            out_ref[width, row, SLOT:, :128] = latent[start : start + 16].astype(BF16)
            rest = jnp.concatenate([latent[start + 16 : start + GROUP], blank], axis=0)
            out_ref[width, row, SLOT:, 128:] = rest.astype(BF16)


def grid_place(odd, row):
    target = row // 16 % 4 * 64 + row // 128 * 16 + row % 16
    return jnp.where(row // 64 % 2 == odd, target, -1)


def patch_body(place_ref, mine_ref, handed_ref, flat_ref, latent_ref):
    core = place_ref[2]
    lane = lax.broadcasted_iota(jnp.int32, (4 * SLOT, 256), 1) % 64
    blocks = [[None] * 4 for _ in range(4)]
    for width in range(4):
        for row in range(4):
            blocks[row][width] = jnp.where(core == 0, mine_ref[width, row], handed_ref[width, row])
    places = [one_hot((512, 256), functools.partial(grid_place, odd)) for odd in range(2)]
    frames = []
    for pair in range(2):
        cut = slice(pair * 128, pair * 128 + 128)
        rows = [
            jnp.concatenate([blocks[row][width][:SLOT, cut] for width in range(4)], axis=1) for row in range(4)
        ]
        rows = jnp.concatenate(rows, axis=0)
        frames += [jnp.dot(rows, place, preferred_element_type=F32) for place in places]
    for time_tap in range(3):
        still = jnp.where(core == 0, frames[time_tap], frames[time_tap + 1])
        left = jnp.where(lane == 0, 0.0, pltpu.roll(still, 1, 1))
        right = jnp.where(lane == 63, 0.0, pltpu.roll(still, 255, 1))
        for col_tap, base in enumerate((left, still, right)):
            slot = (time_tap * 3 + col_tap) * SLOT
            base = base.astype(BF16)
            for row in range(4):
                flat_ref[slot : slot + SLOT, row * 256 : row * 256 + 256] = base[row * SLOT : row * SLOT + SLOT]
    flat_ref[9 * SLOT :, :] = jnp.zeros((BAND - 9 * SLOT, 1024), BF16)
    place = jnp.where(core == 0, places[0], places[1])
    for row in range(4):
        for half, count in ((0, 16), (1, 8)):
            cut = slice(half * 128, half * 128 + 128)
            part = jnp.concatenate([blocks[row][width][SLOT:, cut] for width in range(4)], axis=1)
            part = jnp.dot(part, place, preferred_element_type=F32)[:count]
            latent_ref[half * 16 : half * 16 + count, row * 256 : row * 256 + 256] = part


def main_place(row):
    part = row // SLOT * 6 + row % 6
    return jnp.where(part < 16, row % SLOT // 6 * 16 + part, -1)


def spare_place(tile, row):
    part = row % 6 - 4
    return jnp.where(part >= 0, row // 6 * 16 + part * 7 + tile, -1)


def conv_body(place_ref, flat_ref, latent_ref, mine_ref, handed_ref, out_ref):
    gathered = jnp.where(place_ref[2] == 1, mine_ref[...], handed_ref[...])
    main = jnp.dot(one_hot((3 * SLOT, 256), main_place), gathered[:, :BAND], preferred_element_type=F32)
    spare = [
        jnp.dot(
            one_hot((SLOT, 256), functools.partial(spare_place, tile)),
            gathered[:, BAND:],
            preferred_element_type=F32,
        )
        for tile in range(BAND // 128)
    ]
    last = main[2 * SLOT :] + jnp.concatenate(spare, axis=1)
    weight = jnp.concatenate([main[: 2 * SLOT], last], axis=0).astype(BF16)
    whole = jnp.dot(weight, flat_ref[...], preferred_element_type=F32)
    lane = lax.broadcasted_iota(jnp.int32, (SLOT, 1024), 1)
    total = whole[SLOT : 2 * SLOT]
    total += jnp.where(lane < 64, 0.0, pltpu.roll(whole[:SLOT], 64, 1))
    total += jnp.where(lane < 960, pltpu.roll(whole[2 * SLOT :], 960, 1), 0.0)
    owner = lax.broadcasted_iota(jnp.int32, (SLOT, 1024), 0) // GROUP
    total += jnp.where(owner == place_ref[3], jnp.concatenate([latent_ref[...]] * 4, axis=0), 0.0)
    pieces = [total[:, part * 256 : part * 256 + 256].T for part in range(4)]
    for width in range(4):
        rows = [
            pieces[row // 4][row % 4 * 64 + width * 16 : row % 4 * 64 + width * 16 + 16] for row in range(16)
        ]
        out_ref[width] = jnp.concatenate(rows, axis=0).T.astype(BF16)


def hidden_body(part_ref, out_ref):
    summed = part_ref[0].astype(F32)
    for source in range(1, 4):
        summed += part_ref[source].astype(F32)
    hidden = summed.astype(BF16)
    for target in range(16):
        out_ref[target] = hidden


def fold_body(w_ref, w_out_ref, row_ref, column_ref, score_ref, update_ref, order_ref):
    order = one_hot((384, 384), channel_of)
    order_ref[...] = order
    gain = column_ref[...]
    score = lax.dot_general(
        w_ref[:, :384], w_ref[:, 384:768], (((1,), (1,)), ((), ())), preferred_element_type=F32
    )
    score = (score * (gain * (1.0 / 384.0**0.5)) * row_ref[...]).astype(BF16)
    score = jnp.dot(order, score, preferred_element_type=F32).astype(BF16)
    score = lax.dot_general(score, order, (((1,), (1,)), ((), ())), preferred_element_type=F32)
    score_ref[...] = score.astype(BF16)
    update = jnp.dot(w_ref[:, 768:], w_out_ref[...], preferred_element_type=F32) * gain
    update_ref[...] = jnp.dot(order, update.astype(BF16), preferred_element_type=F32).astype(BF16)


def attend_body(place_ref, block_ref, score_ref, update_ref, order_ref, keep_ref, send_ref):
    own = block_ref[place_ref[3]]
    own = jnp.where(place_ref[1] < 2, own[:, :128], own[:, 128:]).astype(F32).T
    own = jnp.where(place_ref[1] % 2 == 0, own[:64], own[64:])
    own_scale = lax.rsqrt(jnp.mean(own * own, axis=-1, keepdims=True) + 1e-06)
    own = own.astype(BF16)
    query = jnp.dot(own, score_ref[...], preferred_element_type=F32)
    query = (query * own_scale).astype(BF16)
    hidden = jnp.dot(own, order_ref[...], preferred_element_type=F32)
    scales, scores = [], []
    for width in range(4):
        cells = block_ref[width]
        values = cells.astype(F32)
        scale = lax.rsqrt(jnp.mean(values * values, axis=0, keepdims=True) + 1e-06)
        scales.append(scale)
        scores.append(jnp.dot(query, cells, preferred_element_type=F32) * scale)
    peak = functools.reduce(jnp.maximum, [jnp.max(part, axis=-1, keepdims=True) for part in scores])
    total = jnp.zeros((64, 1), F32)
    mixed = jnp.zeros((64, 384), F32)
    for width in range(4):
        powers = jnp.exp(scores[width] - peak)
        total += jnp.sum(powers, axis=-1, keepdims=True)
        powers = (powers * scales[width]).astype(BF16)
        mixed += lax.dot_general(
            powers, block_ref[width], (((1,), (1,)), ((), ())), preferred_element_type=F32
        )
    mixed = (mixed / total).astype(BF16)
    decoded = (hidden + jnp.dot(mixed, update_ref[...], preferred_element_type=F32)).astype(BF16)
    first = place_ref[2] == 0
    keep_ref[...] = jnp.where(first, decoded[:32], decoded[32:])
    send_ref[...] = jnp.where(first, decoded[32:], decoded[:32])


def rms_scale(values, gain):
    mean_sq = jnp.mean(values * values, axis=-1, keepdims=True)
    return values * lax.rsqrt(mean_sq + 1e-06) * gain


def local(latent, norm_gain, conv_weight, attn_gain, w_qkv, w_out):
    channels = 384
    core = lax.axis_index("core")
    place = [lax.axis_index("tm"), lax.axis_index("y"), core, lax.axis_index("width")]
    place = jnp.stack(place).astype(jnp.int32)
    swap = [(0, 1), (1, 0)]
    shape = jax.ShapeDtypeStruct
    cells = latent.reshape(64, channels)
    weight_shape, block_shape = (256, 1024), (16, ROWS, 256)

    def gather_weights(cells, lower, gain, piece):
        weight = lax.all_gather(piece, "tm", axis=0, tiled=True)
        return weight, jnp.zeros(block_shape, BF16)

    def exchange_cells(cells, lower, gain, piece):
        now = jnp.concatenate([cells, lower], axis=0)
        before = lax.ppermute(now, ("tm", "core"), [(2 * i, 2 * i + 2) for i in range(15)])
        blocks = call(block_body, shape((4, 4, ROWS, 256), BF16), [VMEM] * 3)(before, now, gain)
        return jnp.zeros(weight_shape, BF16), lax.all_to_all(blocks.reshape(block_shape), PLANE, 0, 0)

    with jax.named_scope("weights_and_cells"):
        lower = lax.ppermute(cells, "core", [(1, 0)])
        turned = jnp.transpose(conv_weight.reshape(TAPS, channels, GROUP), (0, 2, 1))
        piece = call(weight_body, shape((16, 1024), BF16), [SMEM, VMEM], limit=FIRST_LIMIT)(place, turned)
        weight, blocks = lax.cond(
            core == 1, gather_weights, exchange_cells, cells, lower, norm_gain.reshape(1, channels), piece
        )
    with jax.named_scope("patches"):
        handed_blocks = lax.ppermute(blocks, "core", [(0, 1)])
        handed_weight = lax.ppermute(weight, "core", [(1, 0)])
        grouped = (4, 4, ROWS, 256)
        flat, own = call(
            patch_body, [shape((BAND, 1024), BF16), shape((GROUP, 1024), F32)], [SMEM] + [VMEM] * 2
        )(place, blocks.reshape(grouped), handed_blocks.reshape(grouped))
    with jax.named_scope("conv"):
        parts = call(conv_body, shape((4, SLOT, 256), BF16), [SMEM] + [VMEM] * 4, 700_000_000)(
            place, flat, own, weight, handed_weight
        )
        parts = lax.all_to_all(parts, "width", 0, 0)
    with jax.named_scope("hidden"):
        hidden = call(hidden_body, shape((16, SLOT, 256), BF16), [VMEM])(parts)
        hidden = lax.all_to_all(hidden, PLANE, 0, 0)
    with jax.named_scope("attention"):
        square, half = shape((channels, channels), BF16), shape((32, channels), BF16)
        score, update, order = call(fold_body, [square] * 3, [VMEM] * 4, 600_000_000)(
            w_qkv, w_out, attn_gain.reshape(1, channels), attn_gain.reshape(channels, 1)
        )
        keep, send = call(attend_body, [half, half], [SMEM] + [VMEM] * 4, 200_000_000)(
            place, hidden.reshape(4, channels, 256), score, update, order
        )
        got = lax.ppermute(send, "core", swap)
        out = jnp.where(core == 0, jnp.concatenate([keep, got]), jnp.concatenate([got, keep]))
    return out.reshape(latent.shape)


def solution(mesh):
    devices = mesh.devices.reshape(16, 4, 2, 4)
    fine = Mesh(devices, ("tm", "y", "core", "width"))
    cells = P("tm", ("y", "core"), "width", None)
    in_specs = (cells, P(), P(None, None, None, None, "tm"), P(), P(), P())
    return jax.shard_map(local, mesh=fine, in_specs=in_specs, out_specs=cells, check_vma=False)
```

```python
import functools

import jax
import jax.numpy as jnp
from jax import lax
from jax.experimental import pallas as pl
from jax.experimental.pallas import tpu as pltpu
from jax.sharding import Mesh, PartitionSpec as P

F32 = jnp.float32
BF16 = jnp.bfloat16
TAPS = 27
GROUP = 24
SLOT = 96
ROWS = SLOT + 16
BAND = 896
PLANE = ("width", "y")
VMEM = pl.BlockSpec(memory_space=pltpu.VMEM)
SMEM = pl.BlockSpec(memory_space=pltpu.SMEM)
LIMIT = 12 * 1024 * 1024
FIRST_LIMIT = 55040 * 1024


def call(body, out, specs, flops=1_000_000, moved=1_000_000, scratch=(), limit=LIMIT):
    many = isinstance(out, (tuple, list))
    return pl.pallas_call(
        body,
        out_shape=out,
        in_specs=specs,
        out_specs=[VMEM] * len(out) if many else VMEM,
        scratch_shapes=list(scratch),
        compiler_params=pltpu.CompilerParams(vmem_limit_bytes=limit),
        cost_estimate=pl.CostEstimate(flops=flops, bytes_accessed=moved, transcendentals=0),
    )


def one_hot(shape, column_of):
    row = lax.broadcasted_iota(jnp.int32, (shape[0], 1), 0)
    col = lax.broadcasted_iota(jnp.int32, shape, 1)
    return (col == column_of(row)).astype(F32).astype(BF16)


def channel_of(place):
    return place % SLOT // 6 * GROUP + place // SLOT * 6 + place % 6


def activated(values, gain):
    scaled = rms_scale(values.astype(F32), gain)
    return scaled / (1.0 + jnp.exp(-scaled))


def weight_body(place_ref, weight_ref, piece_ref):
    start = place_ref[3] * SLOT
    pick = one_hot((384, 128), lambda row: jnp.where(row - start < SLOT, row - start, -1))
    rows = jnp.concatenate([weight_ref[tap] for tap in range(TAPS)], axis=0)
    picked = jnp.dot(rows, pick, preferred_element_type=F32)
    upper = place_ref[1] // 2
    picked = jnp.where(upper == 0, picked, pltpu.roll(picked, TAPS * GROUP - 12, 0))
    picked = jnp.where(place_ref[1] % 2 == 0, picked, pltpu.roll(picked, TAPS * GROUP - 6, 0))
    lane = lax.broadcasted_iota(jnp.int32, (8, 128), 1)
    kept = lax.broadcasted_iota(jnp.int32, (8, 128), 0) < 6
    tiles = [jnp.zeros((8, 128), F32) for _ in range(3 * BAND // 128)]
    for row_tap in range(3):
        for slot in range(9):
            tap = slot // 3 * 9 + row_tap * 3 + slot % 3
            value = jnp.where(kept, picked[tap * GROUP : tap * GROUP + 8], 0.0)
            tile, offset = divmod(row_tap * BAND + slot * SLOT, 128)
            value = pltpu.roll(value, offset, 1) if offset else value
            if offset + SLOT > 128:
                tiles[tile] += jnp.where(lane >= offset, value, 0.0)
                tiles[tile + 1] += jnp.where(lane < offset, value, 0.0)
            else:
                tiles[tile] += value
    main, spare = [], [[], []]
    for tile in range(BAND // 128):
        stack = jnp.concatenate([tiles[band * 7 + tile][:6] for band in range(3)], axis=0)
        main.append(stack[:16])
        spare[0].append(stack[16:17])
        spare[1].append(stack[17:])
    spare = jnp.concatenate(spare[0] + spare[1] + [jnp.zeros((2, 128), F32)], axis=0)
    piece_ref[...] = jnp.concatenate(main + [spare], axis=1).astype(BF16)


def activated(values, gain):
    scaled = rms_scale(values.astype(F32), gain)
    return scaled / (1.0 + jnp.exp(-scaled))


def by_frame(ref):
    return jnp.concatenate([ref[0:32], ref[64:96], ref[32:64], ref[96:128]], axis=0)


def block_body(before_ref, now_ref, gain_ref, out_ref):
    now = by_frame(now_ref)
    both = activated(jnp.concatenate([by_frame(before_ref), now], axis=0), gain_ref[...]).T.astype(BF16)
    latent = lax.dot_general(
        one_hot((384, 384), channel_of), now, (((1,), (1,)), ((), ())), preferred_element_type=F32
    )
    blank = jnp.zeros((8, 128), F32)
    for width in range(4):
        for row in range(4):
            start = row * SLOT + width * GROUP
            out_ref[width, row, :SLOT, :] = both[width * SLOT : width * SLOT + SLOT]
            out_ref[width, row, SLOT:, :128] = latent[start : start + 16].astype(BF16)
            rest = jnp.concatenate([latent[start + 16 : start + GROUP], blank], axis=0)
            out_ref[width, row, SLOT:, 128:] = rest.astype(BF16)


def grid_place(odd, row):
    target = row // 16 % 4 * 64 + row // 128 * 16 + row % 16
    return jnp.where(row // 64 % 2 == odd, target, -1)


def patch_body(place_ref, mine_ref, handed_ref, flat_ref, latent_ref):
    core = place_ref[2]
    lane = lax.broadcasted_iota(jnp.int32, (4 * SLOT, 256), 1) % 64
    blocks = [[None] * 4 for _ in range(4)]
    for width in range(4):
        for row in range(4):
            blocks[row][width] = jnp.where(core == 0, mine_ref[width, row], handed_ref[width, row])
    places = [one_hot((512, 256), functools.partial(grid_place, odd)) for odd in range(2)]
    frames = []
    for pair in range(2):
        cut = slice(pair * 128, pair * 128 + 128)
        rows = [
            jnp.concatenate([blocks[row][width][:SLOT, cut] for width in range(4)], axis=1) for row in range(4)
        ]
        rows = jnp.concatenate(rows, axis=0)
        frames += [jnp.dot(rows, place, preferred_element_type=F32) for place in places]
    for time_tap in range(3):
        still = jnp.where(core == 0, frames[time_tap], frames[time_tap + 1])
        left = jnp.where(lane == 0, 0.0, pltpu.roll(still, 1, 1))
        right = jnp.where(lane == 63, 0.0, pltpu.roll(still, 255, 1))
        for col_tap, base in enumerate((left, still, right)):
            slot = (time_tap * 3 + col_tap) * SLOT
            base = base.astype(BF16)
            for row in range(4):
                flat_ref[slot : slot + SLOT, row * 256 : row * 256 + 256] = base[row * SLOT : row * SLOT + SLOT]
    flat_ref[9 * SLOT :, :] = jnp.zeros((BAND - 9 * SLOT, 1024), BF16)
    place = jnp.where(core == 0, places[0], places[1])
    for row in range(4):
        for half, count in ((0, 16), (1, 8)):
            cut = slice(half * 128, half * 128 + 128)
            part = jnp.concatenate([blocks[row][width][SLOT:, cut] for width in range(4)], axis=1)
            part = jnp.dot(part, place, preferred_element_type=F32)[:count]
            latent_ref[half * 16 : half * 16 + count, row * 256 : row * 256 + 256] = part


def main_place(row):
    part = row // SLOT * 6 + row % 6
    return jnp.where(part < 16, row % SLOT // 6 * 16 + part, -1)


def spare_place(tile, row):
    part = row % 6 - 4
    return jnp.where(part >= 0, row // 6 * 16 + part * 7 + tile, -1)


def conv_body(place_ref, flat_ref, latent_ref, mine_ref, handed_ref, out_ref):
    gathered = jnp.where(place_ref[2] == 1, mine_ref[...], handed_ref[...])
    main = jnp.dot(one_hot((3 * SLOT, 256), main_place), gathered[:, :BAND], preferred_element_type=F32)
    spare = [
        jnp.dot(
            one_hot((SLOT, 256), functools.partial(spare_place, tile)),
            gathered[:, BAND:],
            preferred_element_type=F32,
        )
        for tile in range(BAND // 128)
    ]
    last = main[2 * SLOT :] + jnp.concatenate(spare, axis=1)
    weight = jnp.concatenate([main[: 2 * SLOT], last], axis=0).astype(BF16)
    whole = jnp.dot(weight, flat_ref[...], preferred_element_type=F32)
    lane = lax.broadcasted_iota(jnp.int32, (SLOT, 1024), 1)
    total = whole[SLOT : 2 * SLOT]
    total += jnp.where(lane < 64, 0.0, pltpu.roll(whole[:SLOT], 64, 1))
    total += jnp.where(lane < 960, pltpu.roll(whole[2 * SLOT :], 960, 1), 0.0)
    owner = lax.broadcasted_iota(jnp.int32, (SLOT, 1024), 0) // GROUP
    total += jnp.where(owner == place_ref[3], jnp.concatenate([latent_ref[...]] * 4, axis=0), 0.0)
    pieces = [total[:, part * 256 : part * 256 + 256].T for part in range(4)]
    for width in range(4):
        rows = [
            pieces[row // 4][row % 4 * 64 + width * 16 : row % 4 * 64 + width * 16 + 16] for row in range(16)
        ]
        out_ref[width] = jnp.concatenate(rows, axis=0).T.astype(BF16)


def hidden_body(part_ref, out_ref):
    summed = part_ref[0].astype(F32)
    for source in range(1, 4):
        summed += part_ref[source].astype(F32)
    hidden = summed.astype(BF16)
    for target in range(16):
        out_ref[target] = hidden


def fold_body(w_ref, w_out_ref, row_ref, column_ref, score_ref, update_ref, order_ref):
    order = one_hot((384, 384), channel_of)
    order_ref[...] = order
    gain = column_ref[...]
    score = lax.dot_general(
        w_ref[:, :384], w_ref[:, 384:768], (((1,), (1,)), ((), ())), preferred_element_type=F32
    )
    score = (score * (gain * (1.0 / 384.0**0.5)) * row_ref[...]).astype(BF16)
    score = jnp.dot(order, score, preferred_element_type=F32).astype(BF16)
    score = lax.dot_general(score, order, (((1,), (1,)), ((), ())), preferred_element_type=F32)
    score_ref[...] = score.astype(BF16)
    update = jnp.dot(w_ref[:, 768:], w_out_ref[...], preferred_element_type=F32) * gain
    update_ref[...] = jnp.dot(order, update.astype(BF16), preferred_element_type=F32).astype(BF16)


def attend_body(place_ref, block_ref, score_ref, update_ref, order_ref, keep_ref, send_ref):
    own = block_ref[place_ref[3]]
    own = jnp.where(place_ref[1] < 2, own[:, :128], own[:, 128:]).astype(F32).T
    own = jnp.where(place_ref[1] % 2 == 0, own[:64], own[64:])
    own_scale = lax.rsqrt(jnp.mean(own * own, axis=-1, keepdims=True) + 1e-06)
    own = own.astype(BF16)
    query = jnp.dot(own, score_ref[...], preferred_element_type=F32)
    query = (query * own_scale).astype(BF16)
    hidden = jnp.dot(own, order_ref[...], preferred_element_type=F32)
    scales, scores = [], []
    for width in range(4):
        cells = block_ref[width]
        values = cells.astype(F32)
        scale = lax.rsqrt(jnp.mean(values * values, axis=0, keepdims=True) + 1e-06)
        scales.append(scale)
        scores.append(jnp.dot(query, cells, preferred_element_type=F32) * scale)
    peak = functools.reduce(jnp.maximum, [jnp.max(part, axis=-1, keepdims=True) for part in scores])
    total = jnp.zeros((64, 1), F32)
    mixed = jnp.zeros((64, 384), F32)
    for width in range(4):
        powers = jnp.exp(scores[width] - peak)
        total += jnp.sum(powers, axis=-1, keepdims=True)
        powers = (powers * scales[width]).astype(BF16)
        mixed += lax.dot_general(
            powers, block_ref[width], (((1,), (1,)), ((), ())), preferred_element_type=F32
        )
    mixed = (mixed / total).astype(BF16)
    decoded = (hidden + jnp.dot(mixed, update_ref[...], preferred_element_type=F32)).astype(BF16)
    first = place_ref[2] == 0
    keep_ref[...] = jnp.where(first, decoded[:32], decoded[32:])
    send_ref[...] = jnp.where(first, decoded[32:], decoded[:32])


def rms_scale(values, gain):
    mean_sq = jnp.mean(values * values, axis=-1, keepdims=True)
    return values * lax.rsqrt(mean_sq + 1e-06) * gain


def local(latent, norm_gain, conv_weight, attn_gain, w_qkv, w_out):
    channels = 384
    core = lax.axis_index("core")
    place = [lax.axis_index("tm"), lax.axis_index("y"), core, lax.axis_index("width")]
    place = jnp.stack(place).astype(jnp.int32)
    swap = [(0, 1), (1, 0)]
    shape = jax.ShapeDtypeStruct
    cells = latent.reshape(64, channels)
    weight_shape, block_shape = (256, 1024), (16, ROWS, 256)

    def gather_weights(cells, lower, gain, piece):
        weight = lax.all_gather(piece, "tm", axis=0, tiled=True)
        return weight, jnp.zeros(block_shape, BF16)

    def exchange_cells(cells, lower, gain, piece):
        now = jnp.concatenate([cells, lower], axis=0)
        before = lax.ppermute(now, ("tm", "core"), [(2 * i, 2 * i + 2) for i in range(15)])
        blocks = call(block_body, shape((4, 4, ROWS, 256), BF16), [VMEM] * 3)(before, now, gain)
        return jnp.zeros(weight_shape, BF16), lax.all_to_all(blocks.reshape(block_shape), PLANE, 0, 0)

    with jax.named_scope("weights_and_cells"):
        lower = lax.ppermute(cells, "core", [(1, 0)])
        turned = jnp.transpose(conv_weight.reshape(TAPS, channels, GROUP), (0, 2, 1))
        piece = call(weight_body, shape((16, 1024), BF16), [SMEM, VMEM], limit=FIRST_LIMIT)(place, turned)
        weight, blocks = lax.cond(
            core == 1, gather_weights, exchange_cells, cells, lower, norm_gain.reshape(1, channels), piece
        )
    with jax.named_scope("patches"):
        handed_blocks = lax.ppermute(blocks, "core", [(0, 1)])
        handed_weight = lax.ppermute(weight, "core", [(1, 0)])
        grouped = (4, 4, ROWS, 256)
        flat, own = call(
            patch_body, [shape((BAND, 1024), BF16), shape((GROUP, 1024), F32)], [SMEM] + [VMEM] * 2
        )(place, blocks.reshape(grouped), handed_blocks.reshape(grouped))
    with jax.named_scope("conv"):
        parts = call(conv_body, shape((4, SLOT, 256), BF16), [SMEM] + [VMEM] * 4, 700_000_000)(
            place, flat, own, weight, handed_weight
        )
        parts = lax.all_to_all(parts, "width", 0, 0)
    with jax.named_scope("folded_weights"):
        square, half = shape((channels, channels), BF16), shape((32, channels), BF16)
        score, update, order = call(fold_body, [square] * 3, [VMEM] * 4, 600_000_000)(
            w_qkv, w_out, attn_gain.reshape(1, channels), attn_gain.reshape(channels, 1)
        )
        parts, score, update, order = lax.optimization_barrier((parts, score, update, order))
    with jax.named_scope("hidden"):
        hidden = call(hidden_body, shape((16, SLOT, 256), BF16), [VMEM])(parts)
        hidden = lax.all_to_all(hidden, PLANE, 0, 0)
    with jax.named_scope("attention"):
        keep, send = call(attend_body, [half, half], [SMEM] + [VMEM] * 4, 200_000_000)(
            place, hidden.reshape(4, channels, 256), score, update, order
        )
        got = lax.ppermute(send, "core", swap)
        out = jnp.where(core == 0, jnp.concatenate([keep, got]), jnp.concatenate([got, keep]))
    return out.reshape(latent.shape)


def solution(mesh):
    devices = mesh.devices.reshape(16, 4, 2, 4)
    fine = Mesh(devices, ("tm", "y", "core", "width"))
    cells = P("tm", ("y", "core"), "width", None)
    in_specs = (cells, P(), P(None, None, None, None, "tm"), P(), P(), P())
    return jax.shard_map(local, mesh=fine, in_specs=in_specs, out_specs=cells, check_vma=False)
```

```python
import functools

import jax
import jax.numpy as jnp
from jax import lax
from jax.experimental import pallas as pl
from jax.experimental.pallas import tpu as pltpu
from jax.sharding import Mesh, PartitionSpec as P

F32 = jnp.float32
BF16 = jnp.bfloat16
TAPS = 27
GROUP = 24
SLOT = 96
ROWS = SLOT + 16
BAND = 896
PLANE = ("width", "y")
VMEM = pl.BlockSpec(memory_space=pltpu.VMEM)
SMEM = pl.BlockSpec(memory_space=pltpu.SMEM)
LIMIT = 12 * 1024 * 1024
FIRST_LIMIT = 55040 * 1024


def call(body, out, specs, flops=1_000_000, moved=1_000_000, scratch=(), limit=LIMIT):
    many = isinstance(out, (tuple, list))
    return pl.pallas_call(
        body,
        out_shape=out,
        in_specs=specs,
        out_specs=[VMEM] * len(out) if many else VMEM,
        scratch_shapes=list(scratch),
        compiler_params=pltpu.CompilerParams(vmem_limit_bytes=limit),
        cost_estimate=pl.CostEstimate(flops=flops, bytes_accessed=moved, transcendentals=0),
    )


def one_hot(shape, column_of):
    row = lax.broadcasted_iota(jnp.int32, (shape[0], 1), 0)
    col = lax.broadcasted_iota(jnp.int32, shape, 1)
    return (col == column_of(row)).astype(F32).astype(BF16)


def channel_of(place):
    return place % SLOT // 6 * GROUP + place // SLOT * 6 + place % 6


def activated(values, gain):
    scaled = rms_scale(values.astype(F32), gain)
    return scaled / (1.0 + jnp.exp(-scaled))


def weight_body(place_ref, weight_ref, piece_ref):
    start = place_ref[3] * SLOT
    pick = one_hot((384, 128), lambda row: jnp.where(row - start < SLOT, row - start, -1))
    rows = jnp.concatenate([weight_ref[tap] for tap in range(TAPS)], axis=0)
    picked = jnp.dot(rows, pick, preferred_element_type=F32)
    upper = place_ref[1] // 2
    picked = jnp.where(upper == 0, picked, pltpu.roll(picked, TAPS * GROUP - 12, 0))
    picked = jnp.where(place_ref[1] % 2 == 0, picked, pltpu.roll(picked, TAPS * GROUP - 6, 0))
    lane = lax.broadcasted_iota(jnp.int32, (8, 128), 1)
    kept = lax.broadcasted_iota(jnp.int32, (8, 128), 0) < 6
    tiles = [jnp.zeros((8, 128), F32) for _ in range(3 * BAND // 128)]
    for row_tap in range(3):
        for slot in range(9):
            tap = slot // 3 * 9 + row_tap * 3 + slot % 3
            value = jnp.where(kept, picked[tap * GROUP : tap * GROUP + 8], 0.0)
            tile, offset = divmod(row_tap * BAND + slot * SLOT, 128)
            value = pltpu.roll(value, offset, 1) if offset else value
            if offset + SLOT > 128:
                tiles[tile] += jnp.where(lane >= offset, value, 0.0)
                tiles[tile + 1] += jnp.where(lane < offset, value, 0.0)
            else:
                tiles[tile] += value
    main, spare = [], [[], []]
    for tile in range(BAND // 128):
        stack = jnp.concatenate([tiles[band * 7 + tile][:6] for band in range(3)], axis=0)
        main.append(stack[:16])
        spare[0].append(stack[16:17])
        spare[1].append(stack[17:])
    spare = jnp.concatenate(spare[0] + spare[1] + [jnp.zeros((2, 128), F32)], axis=0)
    piece_ref[...] = jnp.concatenate(main + [spare], axis=1).astype(BF16)


def activated(values, gain):
    scaled = rms_scale(values.astype(F32), gain)
    return scaled / (1.0 + jnp.exp(-scaled))


def by_frame(ref):
    return jnp.concatenate([ref[0:32], ref[64:96], ref[32:64], ref[96:128]], axis=0)


def block_body(before_ref, now_ref, gain_ref, out_ref):
    now = by_frame(now_ref)
    both = activated(jnp.concatenate([by_frame(before_ref), now], axis=0), gain_ref[...]).T.astype(BF16)
    latent = lax.dot_general(
        one_hot((384, 384), channel_of), now, (((1,), (1,)), ((), ())), preferred_element_type=F32
    )
    blank = jnp.zeros((8, 128), F32)
    for width in range(4):
        for row in range(4):
            start = row * SLOT + width * GROUP
            out_ref[width, row, :SLOT, :] = both[width * SLOT : width * SLOT + SLOT]
            out_ref[width, row, SLOT:, :128] = latent[start : start + 16].astype(BF16)
            rest = jnp.concatenate([latent[start + 16 : start + GROUP], blank], axis=0)
            out_ref[width, row, SLOT:, 128:] = rest.astype(BF16)


def grid_place(odd, row):
    target = row // 16 % 4 * 64 + row // 128 * 16 + row % 16
    return jnp.where(row // 64 % 2 == odd, target, -1)


def patch_body(place_ref, mine_ref, handed_ref, flat_ref, latent_ref, dense_ref):
    dense_ref[: 3 * SLOT, :] = one_hot((3 * SLOT, 256), main_place)
    for tile in range(BAND // 128):
        start = (3 + tile) * SLOT
        dense_ref[start : start + SLOT, :] = one_hot((SLOT, 256), functools.partial(spare_place, tile))
    core = place_ref[2]
    lane = lax.broadcasted_iota(jnp.int32, (4 * SLOT, 256), 1) % 64
    blocks = [[None] * 4 for _ in range(4)]
    for width in range(4):
        for row in range(4):
            blocks[row][width] = jnp.where(core == 0, mine_ref[width, row], handed_ref[width, row])
    places = [one_hot((512, 256), functools.partial(grid_place, odd)) for odd in range(2)]
    frames = []
    for pair in range(2):
        cut = slice(pair * 128, pair * 128 + 128)
        rows = [
            jnp.concatenate([blocks[row][width][:SLOT, cut] for width in range(4)], axis=1) for row in range(4)
        ]
        rows = jnp.concatenate(rows, axis=0)
        frames += [jnp.dot(rows, place, preferred_element_type=F32) for place in places]
    for time_tap in range(3):
        still = jnp.where(core == 0, frames[time_tap], frames[time_tap + 1])
        left = jnp.where(lane == 0, 0.0, pltpu.roll(still, 1, 1))
        right = jnp.where(lane == 63, 0.0, pltpu.roll(still, 255, 1))
        for col_tap, base in enumerate((left, still, right)):
            slot = (time_tap * 3 + col_tap) * SLOT
            base = base.astype(BF16)
            for row in range(4):
                flat_ref[slot : slot + SLOT, row * 256 : row * 256 + 256] = base[row * SLOT : row * SLOT + SLOT]
    flat_ref[9 * SLOT :, :] = jnp.zeros((BAND - 9 * SLOT, 1024), BF16)
    place = jnp.where(core == 0, places[0], places[1])
    for row in range(4):
        for half, count in ((0, 16), (1, 8)):
            cut = slice(half * 128, half * 128 + 128)
            part = jnp.concatenate([blocks[row][width][SLOT:, cut] for width in range(4)], axis=1)
            part = jnp.dot(part, place, preferred_element_type=F32)[:count]
            latent_ref[half * 16 : half * 16 + count, row * 256 : row * 256 + 256] = part


def main_place(row):
    part = row // SLOT * 6 + row % 6
    return jnp.where(part < 16, row % SLOT // 6 * 16 + part, -1)


def spare_place(tile, row):
    part = row % 6 - 4
    return jnp.where(part >= 0, row // 6 * 16 + part * 7 + tile, -1)


def conv_body(place_ref, flat_ref, latent_ref, dense_ref, mine_ref, handed_ref, out_ref):
    gathered = jnp.where(place_ref[2] == 1, mine_ref[...], handed_ref[...])
    main = jnp.dot(dense_ref[: 3 * SLOT, :], gathered[:, :BAND], preferred_element_type=F32)
    spare = [
        jnp.dot(
            dense_ref[(3 + tile) * SLOT : (4 + tile) * SLOT, :],
            gathered[:, BAND:],
            preferred_element_type=F32,
        )
        for tile in range(BAND // 128)
    ]
    last = main[2 * SLOT :] + jnp.concatenate(spare, axis=1)
    weight = jnp.concatenate([main[: 2 * SLOT], last], axis=0).astype(BF16)
    whole = jnp.dot(weight, flat_ref[...], preferred_element_type=F32)
    lane = lax.broadcasted_iota(jnp.int32, (SLOT, 1024), 1)
    total = whole[SLOT : 2 * SLOT]
    total += jnp.where(lane < 64, 0.0, pltpu.roll(whole[:SLOT], 64, 1))
    total += jnp.where(lane < 960, pltpu.roll(whole[2 * SLOT :], 960, 1), 0.0)
    owner = lax.broadcasted_iota(jnp.int32, (SLOT, 1024), 0) // GROUP
    total += jnp.where(owner == place_ref[3], jnp.concatenate([latent_ref[...]] * 4, axis=0), 0.0)
    pieces = [total[:, part * 256 : part * 256 + 256].T for part in range(4)]
    for width in range(4):
        rows = [
            pieces[row // 4][row % 4 * 64 + width * 16 : row % 4 * 64 + width * 16 + 16] for row in range(16)
        ]
        out_ref[width] = jnp.concatenate(rows, axis=0).T.astype(BF16)


def hidden_body(part_ref, out_ref):
    summed = part_ref[0].astype(F32)
    for source in range(1, 4):
        summed += part_ref[source].astype(F32)
    hidden = summed.astype(BF16)
    for target in range(16):
        out_ref[target] = hidden


def fold_body(w_ref, w_out_ref, row_ref, column_ref, score_ref, update_ref, order_ref):
    order = one_hot((384, 384), channel_of)
    order_ref[...] = order
    gain = column_ref[...]
    score = lax.dot_general(
        w_ref[:, :384], w_ref[:, 384:768], (((1,), (1,)), ((), ())), preferred_element_type=F32
    )
    score = (score * (gain * (1.0 / 384.0**0.5)) * row_ref[...]).astype(BF16)
    score = jnp.dot(order, score, preferred_element_type=F32).astype(BF16)
    score = lax.dot_general(score, order, (((1,), (1,)), ((), ())), preferred_element_type=F32)
    score_ref[...] = score.astype(BF16)
    update = jnp.dot(w_ref[:, 768:], w_out_ref[...], preferred_element_type=F32) * gain
    update_ref[...] = jnp.dot(order, update.astype(BF16), preferred_element_type=F32).astype(BF16)


def attend_body(place_ref, block_ref, score_ref, update_ref, order_ref, keep_ref, send_ref):
    own = block_ref[place_ref[3]]
    own = jnp.where(place_ref[1] < 2, own[:, :128], own[:, 128:]).astype(F32).T
    own = jnp.where(place_ref[1] % 2 == 0, own[:64], own[64:])
    own_scale = lax.rsqrt(jnp.mean(own * own, axis=-1, keepdims=True) + 1e-06)
    own = own.astype(BF16)
    query = jnp.dot(own, score_ref[...], preferred_element_type=F32)
    query = (query * own_scale).astype(BF16)
    hidden = jnp.dot(own, order_ref[...], preferred_element_type=F32)
    scales, scores = [], []
    for width in range(4):
        cells = block_ref[width]
        values = cells.astype(F32)
        scale = lax.rsqrt(jnp.mean(values * values, axis=0, keepdims=True) + 1e-06)
        scales.append(scale)
        scores.append(jnp.dot(query, cells, preferred_element_type=F32) * scale)
    peak = functools.reduce(jnp.maximum, [jnp.max(part, axis=-1, keepdims=True) for part in scores])
    total = jnp.zeros((64, 1), F32)
    mixed = jnp.zeros((64, 384), F32)
    for width in range(4):
        powers = jnp.exp(scores[width] - peak)
        total += jnp.sum(powers, axis=-1, keepdims=True)
        powers = (powers * scales[width]).astype(BF16)
        mixed += lax.dot_general(
            powers, block_ref[width], (((1,), (1,)), ((), ())), preferred_element_type=F32
        )
    mixed = (mixed / total).astype(BF16)
    decoded = (hidden + jnp.dot(mixed, update_ref[...], preferred_element_type=F32)).astype(BF16)
    first = place_ref[2] == 0
    keep_ref[...] = jnp.where(first, decoded[:32], decoded[32:])
    send_ref[...] = jnp.where(first, decoded[32:], decoded[:32])


def rms_scale(values, gain):
    mean_sq = jnp.mean(values * values, axis=-1, keepdims=True)
    return values * lax.rsqrt(mean_sq + 1e-06) * gain


def local(latent, norm_gain, conv_weight, attn_gain, w_qkv, w_out):
    channels = 384
    core = lax.axis_index("core")
    place = [lax.axis_index("tm"), lax.axis_index("y"), core, lax.axis_index("width")]
    place = jnp.stack(place).astype(jnp.int32)
    swap = [(0, 1), (1, 0)]
    shape = jax.ShapeDtypeStruct
    cells = latent.reshape(64, channels)
    weight_shape, block_shape = (256, 1024), (16, ROWS, 256)

    def gather_weights(cells, lower, gain, piece):
        weight = lax.all_gather(piece, "tm", axis=0, tiled=True)
        return weight, jnp.zeros(block_shape, BF16)

    def exchange_cells(cells, lower, gain, piece):
        now = jnp.concatenate([cells, lower], axis=0)
        before = lax.ppermute(now, ("tm", "core"), [(2 * i, 2 * i + 2) for i in range(15)])
        blocks = call(block_body, shape((4, 4, ROWS, 256), BF16), [VMEM] * 3)(before, now, gain)
        return jnp.zeros(weight_shape, BF16), lax.all_to_all(blocks.reshape(block_shape), PLANE, 0, 0)

    with jax.named_scope("weights_and_cells"):
        lower = lax.ppermute(cells, "core", [(1, 0)])
        turned = jnp.transpose(conv_weight.reshape(TAPS, channels, GROUP), (0, 2, 1))
        piece = call(weight_body, shape((16, 1024), BF16), [SMEM, VMEM], limit=FIRST_LIMIT)(place, turned)
        weight, blocks = lax.cond(
            core == 1, gather_weights, exchange_cells, cells, lower, norm_gain.reshape(1, channels), piece
        )
    with jax.named_scope("patches"):
        handed_blocks = lax.ppermute(blocks, "core", [(0, 1)])
        handed_weight = lax.ppermute(weight, "core", [(1, 0)])
        grouped = (4, 4, ROWS, 256)
        flat, own, dense = call(
            patch_body, [shape((BAND, 1024), BF16), shape((GROUP, 1024), F32), shape((10 * SLOT, 256), BF16)],
            [SMEM] + [VMEM] * 2,
        )(place, blocks.reshape(grouped), handed_blocks.reshape(grouped))
    with jax.named_scope("conv"):
        parts = call(conv_body, shape((4, SLOT, 256), BF16), [SMEM] + [VMEM] * 5, 700_000_000)(
            place, flat, own, dense, weight, handed_weight
        )
        parts = lax.all_to_all(parts, "width", 0, 0)
    with jax.named_scope("folded_weights"):
        square, half = shape((channels, channels), BF16), shape((32, channels), BF16)
        score, update, order = call(fold_body, [square] * 3, [VMEM] * 4, 600_000_000)(
            w_qkv, w_out, attn_gain.reshape(1, channels), attn_gain.reshape(channels, 1)
        )
        parts, score, update, order = lax.optimization_barrier((parts, score, update, order))
    with jax.named_scope("hidden"):
        hidden = call(hidden_body, shape((16, SLOT, 256), BF16), [VMEM])(parts)
        hidden = lax.all_to_all(hidden, PLANE, 0, 0)
    with jax.named_scope("attention"):
        keep, send = call(attend_body, [half, half], [SMEM] + [VMEM] * 4, 200_000_000)(
            place, hidden.reshape(4, channels, 256), score, update, order
        )
        got = lax.ppermute(send, "core", swap)
        out = jnp.where(core == 0, jnp.concatenate([keep, got]), jnp.concatenate([got, keep]))
    return out.reshape(latent.shape)


def solution(mesh):
    devices = mesh.devices.reshape(16, 4, 2, 4)
    fine = Mesh(devices, ("tm", "y", "core", "width"))
    cells = P("tm", ("y", "core"), "width", None)
    in_specs = (cells, P(), P(None, None, None, None, "tm"), P(), P(), P())
    return jax.shard_map(local, mesh=fine, in_specs=in_specs, out_specs=cells, check_vma=False)
```
